256 devices in a mesh: seq: 16 (over z, core), head: 4 (over x), dp: 4 (over y).
Axes of the slice: x: 4, y: 4, z: 8, core: 2. Of those that a mesh axis runs over, the one named last changes fastest.
Arguments:
- self_queries: bfloat16 [4, 2048, 2560], P('dp', ('seq', 'head')), may hold values from -8 to 8
- self_keys: bfloat16 [4, 2048, 2560], P('dp', ('seq', 'head')), may hold values from -4 to 4
- self_values: bfloat16 [4, 2048, 2560], P('dp', ('seq', 'head')), may hold values from -6 to 6
- self_cotangent: bfloat16 [4, 2048, 2560], P('dp', ('seq', 'head')), may hold values from -6 to 6
- text_queries: bfloat16 [4, 4096, 2560], P('dp', 'seq', 'head'), may hold values from -8 to 8
- memory_keys: bfloat16 [4, 2048, 2560], P('dp', 'seq', 'head'), may hold values from -4 to 4
- memory_values: bfloat16 [4, 2048, 2560], P('dp', 'seq', 'head'), may hold values from -6 to 6
- text_cotangent: bfloat16 [4, 4096, 2560], P('dp', 'seq', 'head'), may hold values from -6 to 6
- slopes: float32 [2, 20], P(None, 'head'), may hold values from 0.01 to 0.3
- page_counts: int32 [4, 4], P('dp'), may hold values from 1 to 1024, as said below
- page_cols: int32 [4, 4], P('dp'), may hold values from 4 to 64
- text_page: int32 [4, 4096], P('dp'), may hold values from 0 to 3, as said below
Outputs:
- self_query_grad: bfloat16 [4, 2048, 2560], P('dp', ('seq', 'head'))
- self_key_grad: bfloat16 [4, 2048, 2560], P('dp', ('seq', 'head'))
- self_value_grad: bfloat16 [4, 2048, 2560], P('dp', ('seq', 'head'))
- slope_grad: float32 [2, 20], P(None, 'head')
- text_query_grad: bfloat16 [4, 4096, 2560], P('dp', 'seq', 'head')
- memory_key_grad: bfloat16 [4, 2048, 2560], P('dp', 'seq', 'head')
- memory_value_grad: bfloat16 [4, 2048, 2560], P('dp', 'seq', 'head')
The draws below stay inside these ranges and needn't reach their ends.
Inputs may be any that keep to these rules, and one draw needn't show every extreme that they name: `page_counts`: each pack's counts sum to 2048; one page of every pack has exactly 1024 patches. `text_page`: never falls along a pack's text rows; every page has at least one text row.
All inputs are finite; a program needn't handle non-finite values.
Results may differ from the reference program's by a relative error of at most 0.006.
Values may be sent and summed in bfloat16 or wider, within the bound.
No kernel may reach another device: no remote copies, remote signals or barrier semaphores. Data moves between devices by JAX's collectives and lax.ppermute only.
A program may use at most 128 MiB of HBM per device.

```python
import math
import jax
import jax.numpy as jnp
from jax import lax

HEADS = 20
HS = 128
PAGES = 4
NP = 2048
TEXT = 4096
PACKS = 4
HD = 2560


def pack_layout(key):
    big_page = NP // 2
    rest_total = NP - big_page
    cut_key = jax.random.fold_in(key, 11)
    place_key = jax.random.fold_in(key, 12)
    text_key = jax.random.fold_in(key, 13)
    cuts = jnp.sort(jax.random.permutation(cut_key, rest_total - 1)[:PAGES - 2] + 1).astype(jnp.int32)
    edges = jnp.concatenate([jnp.zeros((1,), jnp.int32), cuts, jnp.full((1,), rest_total, jnp.int32)])
    smaller = (edges[1:] - edges[:-1]).astype(jnp.int32)
    placed = jax.random.randint(place_key, (), 0, PAGES)
    positions = jnp.arange(PAGES, dtype=jnp.int32)
    padded = jnp.concatenate([smaller, jnp.zeros((1,), jnp.int32)])
    source = jnp.maximum(jnp.where(positions < placed, positions, positions - 1), 0)
    counts = jnp.where(positions == placed, big_page, padded[source])
    text_cuts = jnp.sort(jax.random.permutation(text_key, TEXT - 1)[:PAGES - 1] + 1).astype(jnp.int32)
    text_rows = jnp.arange(TEXT, dtype=jnp.int32)
    text_ids = jnp.sum((text_rows[:, None] >= text_cuts[None, :]).astype(jnp.int32), axis=1)
    return (counts.astype(jnp.int32), text_ids.astype(jnp.int32))


def all_layouts(key):

    def one_pack(pack_index):
        return pack_layout(jax.random.fold_in(key, 1000 + pack_index))
    return jax.vmap(one_pack)(jnp.arange(PACKS))


def paired_keys(key, salt):
    base_key = jax.random.fold_in(key, salt)
    return jax.random.truncated_normal(base_key, -3.5, 3.5, (PACKS, NP, HEADS * HS), jnp.float32)


def draw_self_keys(key, part):
    return paired_keys(key, 21).astype(jnp.bfloat16)


def draw_self_queries(key, part):
    key_table = paired_keys(key, 21)
    drawn_rows = jax.random.truncated_normal(jax.random.fold_in(key, 22), -3.5, 3.5, key_table.shape, jnp.float32)
    return drawn_rows.astype(jnp.bfloat16)


def draw_memory_keys(key, part):
    return paired_keys(key, 31).astype(jnp.bfloat16)


def draw_text_queries(key, part):
    drawn_rows = jax.random.truncated_normal(jax.random.fold_in(key, 32), -3.5, 3.5, (PACKS, TEXT, HEADS * HS), jnp.float32)
    return drawn_rows.astype(jnp.bfloat16)


def draw_page_counts(key, part):
    return all_layouts(key)[0]


def draw_text_page(key, part):
    return all_layouts(key)[1]


def with_ends(values, key, least, largest):
    shape = values.shape
    spot = [jax.random.randint(jax.random.fold_in(key, axis), (), 0, shape[axis]) for axis in range(len(shape))]
    values = values.at[tuple(spot)].set(least)
    longest = shape.index(max(shape))
    spot[longest] = (spot[longest] + 1) % shape[longest]
    return values.at[tuple(spot)].set(largest)


def block_levels(rng, extent, cuts, smallest, high):
    gain, own = 1.0, jax.random.fold_in(rng, 6)
    for axis_at, shards_of in cuts:
        heights = jnp.exp(jax.random.uniform(jax.random.fold_in(own, axis_at), (shards_of,), jnp.float32, smallest / len(cuts), high / len(cuts)))
        gain = gain * jnp.repeat(heights, extent[axis_at] // shards_of).reshape([-1 if axis == axis_at else 1 for axis in range(len(extent))])
    return gain


def scatter_about(stream_key, dims, scale, reach, shards=(), held_as=jnp.bfloat16):
    loudness = block_levels(stream_key, dims, shards, -0.22, 0.18) if shards else 1.0
    values = jax.random.normal(stream_key, dims, jnp.float32) * scale * loudness
    return jnp.minimum(jnp.maximum(values, -reach), reach).astype(held_as)


def setup_inputs(seed: int = 0) -> dict:
    seeds = jax.random.split(jax.random.key(seed), 13)
    self_queries = draw_self_queries(jax.random.fold_in(seeds[12], 71), 0)
    self_keys = draw_self_keys(jax.random.fold_in(seeds[12], 71), 0)
    self_values = scatter_about(seeds[2], (PACKS, NP, HD), 1.0, 6.0, ((0, 4), (1, 64)))
    self_cotangent = scatter_about(seeds[3], (PACKS, NP, HD), 1.0, 6.0, ((0, 4), (1, 64)))
    text_queries = draw_text_queries(jax.random.fold_in(seeds[12], 71), 0)
    memory_keys = draw_memory_keys(jax.random.fold_in(seeds[12], 71), 0)
    memory_values = scatter_about(seeds[6], (PACKS, NP, HD), 1.0, 6.0, ((0, 4), (1, 16), (2, 4)))
    text_cotangent = scatter_about(seeds[7], (PACKS, TEXT, HD), 1.0, 6.0, ((0, 4), (1, 16), (2, 4)))
    slopes = jnp.clip(jnp.exp(math.log(0.3) - 3.4011974 * jax.random.uniform(seeds[8], (2, HEADS), jnp.float32) ** block_levels(seeds[8], (2, HEADS), ((1, 4),), -0.2, 0.2)), 0.01, 0.3)
    page_counts = draw_page_counts(jax.random.fold_in(seeds[12], 71), 0)
    page_cols = with_ends(jax.random.randint(seeds[10], (PACKS, PAGES), 4, 65), jax.random.fold_in(seeds[10], 1), 4, 64).astype(jnp.int32)
    text_page = draw_text_page(jax.random.fold_in(seeds[12], 71), 0)
    return {"self_queries": self_queries, "self_keys": self_keys, "self_values": self_values, "self_cotangent": self_cotangent, "text_queries": text_queries, "memory_keys": memory_keys, "memory_values": memory_values, "text_cotangent": text_cotangent, "slopes": slopes, "page_counts": page_counts, "page_cols": page_cols, "text_page": text_page}


MASK_FILL = -1e30


def page_layout(counts, widths, patch_total):
    page_ends = jnp.cumsum(counts).astype(jnp.int32)
    starts = (page_ends - counts).astype(jnp.int32)
    positions = jnp.arange(patch_total, dtype=jnp.int32)
    page_ids = jnp.sum((positions[:, None] >= page_ends[None, :]).astype(jnp.int32), axis=1).astype(jnp.int32)
    one_hot = page_ids[:, None] == jnp.arange(counts.shape[0], dtype=jnp.int32)[None, :]
    page_start = jnp.sum(jnp.where(one_hot, starts[None, :], 0), axis=1).astype(jnp.int32)
    page_width = jnp.sum(jnp.where(one_hot, widths[None, :], 0), axis=1).astype(jnp.int32)
    offsets = (positions - page_start).astype(jnp.int32)
    return page_ids, (offsets // page_width).astype(jnp.int32), (offsets % page_width).astype(jnp.int32)


def attend(queries, key_rows, value_rows, grad_rows, logit_bias):
    inv_root = queries.shape[1] ** -0.5
    scores = jnp.dot(queries, key_rows.T, preferred_element_type=jnp.float32) * inv_root + logit_bias
    row_max = jnp.max(scores, axis=1, keepdims=True)
    weights = jnp.exp(scores - row_max)
    row_total = jnp.sum(weights, axis=1, keepdims=True)
    softmax_w = weights / row_total
    grad_probs = jnp.dot(grad_rows, value_rows.T, preferred_element_type=jnp.float32)
    row_delta = jnp.sum(softmax_w * grad_probs, axis=1, keepdims=True)
    grad_scores = softmax_w * (grad_probs - row_delta)
    grad_scores_b = grad_scores.astype(jnp.bfloat16)
    query_grad = jnp.dot(grad_scores_b, key_rows, preferred_element_type=jnp.float32) * inv_root
    key_grad = jnp.dot(grad_scores_b.T, queries, preferred_element_type=jnp.float32) * inv_root
    value_grad = jnp.dot(softmax_w.astype(jnp.bfloat16).T, grad_rows, preferred_element_type=jnp.float32)
    return query_grad.astype(jnp.bfloat16), key_grad.astype(jnp.bfloat16), value_grad.astype(jnp.bfloat16), grad_scores


def by_heads(matrix, head_count):
    return jnp.transpose(matrix.reshape(matrix.shape[0], head_count, -1), (1, 0, 2))


def from_heads(stacked):
    return jnp.transpose(stacked, (1, 0, 2)).reshape(stacked.shape[1], -1)


def reference(self_queries, self_keys, self_values, self_cotangent, text_queries, memory_keys, memory_values, text_cotangent, slopes, page_counts, page_cols, text_page):
    head_count = slopes.shape[1]
    self_dq_list = []
    self_dk_list = []
    self_dv_list = []
    text_dq_list = []
    memory_dk_list = []
    memory_dv_list = []
    slope_total = jnp.zeros((2, head_count), jnp.float32)
    for pack_index in range(PACKS):
        page_ids, row_ids, col_ids = page_layout(page_counts[pack_index], page_cols[pack_index], NP)
        row_gap = jnp.abs(row_ids[:, None] - row_ids[None, :]).astype(jnp.float32)
        col_gap = jnp.abs(col_ids[:, None] - col_ids[None, :]).astype(jnp.float32)
        same_page = page_ids[:, None] == page_ids[None, :]

        def self_head(inputs):
            queries, key_rows, value_rows, grad_rows, slope_row, slope_col = inputs
            decay = -(slope_row * row_gap + slope_col * col_gap)
            logit_bias = jnp.where(same_page, decay, MASK_FILL)
            query_grad, key_grad, value_grad, grad_scores = attend(queries, key_rows, value_rows, grad_rows, logit_bias)
            slope_terms = -jnp.stack([jnp.sum(grad_scores * row_gap), jnp.sum(grad_scores * col_gap)])
            return query_grad, key_grad, value_grad, slope_terms

        self_out = lax.map(self_head, (by_heads(self_queries[pack_index], head_count), by_heads(self_keys[pack_index], head_count), by_heads(self_values[pack_index], head_count), by_heads(self_cotangent[pack_index], head_count), slopes[0], slopes[1]))
        self_dq_list.append(from_heads(self_out[0]))
        self_dk_list.append(from_heads(self_out[1]))
        self_dv_list.append(from_heads(self_out[2]))
        slope_total = slope_total + self_out[3].T

        text_same = text_page[pack_index][:, None] == page_ids[None, :]
        cross_bias = jnp.where(text_same, jnp.zeros((), jnp.float32), jnp.full((), MASK_FILL, jnp.float32))

        def cross_head(inputs):
            queries, key_rows, value_rows, grad_rows = inputs
            query_grad, key_grad, value_grad, grad_scores = attend(queries, key_rows, value_rows, grad_rows, cross_bias)
            return query_grad, key_grad, value_grad

        cross_out = lax.map(cross_head, (by_heads(text_queries[pack_index], head_count), by_heads(memory_keys[pack_index], head_count), by_heads(memory_values[pack_index], head_count), by_heads(text_cotangent[pack_index], head_count)))
        text_dq_list.append(from_heads(cross_out[0]))
        memory_dk_list.append(from_heads(cross_out[1]))
        memory_dv_list.append(from_heads(cross_out[2]))
    slope_grad = slope_total / NP
    return (jnp.stack(self_dq_list), jnp.stack(self_dk_list), jnp.stack(self_dv_list), slope_grad, jnp.stack(text_dq_list), jnp.stack(memory_dk_list), jnp.stack(memory_dv_list))
```

```python
import functools
import jax
import jax.numpy as jnp
from jax import lax
from jax.experimental import pallas as pl
from jax.experimental.pallas import tpu as pltpu
from jax.sharding import PartitionSpec as P

MASK_FILL = -1e30
LOG2E = 1.4426950408889634
BF = jnp.bfloat16
F32 = jnp.float32

HEADS = 5
TEXT_TASKS = 10
TASKS = 16
BLK = 128
HS = 128
QB = 256
NARROW = 9


def vmem_call(body, out_shapes, **kw):
    return pl.pallas_call(
        body,
        out_shape=out_shapes,
        compiler_params=pltpu.CompilerParams(vmem_limit_bytes=48 * 2**20),
        **kw,
    )


def pack_self(q_ref, k_ref, v_ref, g_ref, out_ref):
    for a, ref in enumerate((q_ref, k_ref, v_ref, g_ref)):
        for x in range(4):
            for h in range(HEADS):
                c = (x * HEADS + h) * HS
                out_ref[x, h, a] = ref[0, :, c : c + HS]


def pack_tasks(tq_ref, mk_ref, mv_ref, tg_ref, self_ref, out_ref):
    for h in range(HEADS):
        cols = slice(h * HS, (h + 1) * HS)
        for j in range(2):
            t = 2 * h + j
            rows = slice(j * BLK, (j + 1) * BLK)
            out_ref[t, 0] = tq_ref[0, rows, cols]
            out_ref[t, 1] = mk_ref[0, :, cols]
            out_ref[t, 2] = mv_ref[0, :, cols]
            out_ref[t, 3] = tg_ref[0, rows, cols]
        for a in range(4):
            for x in range(4):
                out_ref[TEXT_TASKS + h, a, x * 32 : (x + 1) * 32] = self_ref[x, h, a]
    out_ref[TASKS - 1] = jnp.zeros((4, BLK, HS), BF)


def unpack_tasks(in_ref, tq_ref, mk_ref, mv_ref, self_ref):
    for h in range(HEADS):
        cols = slice(h * HS, (h + 1) * HS)
        for j in range(2):
            tq_ref[0, j * BLK : (j + 1) * BLK, cols] = in_ref[2 * h + j, 0]
        mk = in_ref[2 * h, 1].astype(F32) + in_ref[2 * h + 1, 1].astype(F32)
        mv = in_ref[2 * h, 2].astype(F32) + in_ref[2 * h + 1, 2].astype(F32)
        mk_ref[0, :, cols] = mk.astype(BF)
        mv_ref[0, :, cols] = mv.astype(BF)
        for a in range(3):
            for x in range(4):
                self_ref[x, h, a] = in_ref[TEXT_TASKS + h, a, x * 32 : (x + 1) * 32]


def unpack_self(in_ref, q_ref, k_ref, v_ref):
    for a, ref in enumerate((q_ref, k_ref, v_ref)):
        for x in range(4):
            for h in range(HEADS):
                c = (x * HEADS + h) * HS
                ref[0, :, c : c + HS] = in_ref[x, h, a]


def attend(
    win_ref, ka_ref, kb_ref, kp_ref, qi_ref, in_ref, out_ref, slope_ref,
    k_buf, v_buf, t_buf, d_buf, ds_buf, dk_acc, dv_acc,
):
    inv_root = HS ** (-0.5)
    blocks = TASKS * BLK // QB
    per = QB // BLK
    for s in range(TASKS):
        k_buf[s * BLK : (s + 1) * BLK] = in_ref[s, 1]
        v_buf[s * BLK : (s + 1) * BLK] = in_ref[s, 2]
    dk_acc[...] = jnp.zeros_like(dk_acc)
    dv_acc[...] = jnp.zeros_like(dv_acc)
    slope_ref[...] = jnp.zeros_like(slope_ref)
    nt = (((1,), (1,)), ((), ()))
    tn = (((0,), (0,)), ((), ()))

    def wide_lanes(tile):
        return jnp.concatenate([tile] * per, axis=1)

    def fold(x, op):
        return op(x.reshape(BLK // 8, 8, QB), axis=0)

    def work(b, start, tiles):
        q = jnp.concatenate([in_ref[per * b + i, 0] for i in range(per)], axis=0)
        g = jnp.concatenate([in_ref[per * b + i, 3] for i in range(per)], axis=0)
        at = pl.ds(pl.multiple_of(b * QB, QB), QB)
        qa, qb, qp = (qi_ref[i : i + 1, at] for i in range(3))

        def rows(t):
            return pl.ds(pl.multiple_of(start + t * BLK, BLK), BLK)

        top = jnp.full((8, QB), -jnp.inf, F32)
        for t in range(tiles):
            r = rows(t)
            s = lax.dot_general(k_buf[r], q, nt, preferred_element_type=F32)
            d_buf[t * BLK : (t + 1) * BLK] = lax.dot_general(
                v_buf[r], g, nt, preferred_element_type=F32
            )
            gap = jnp.abs(wide_lanes(ka_ref[r]) - qa) + jnp.abs(wide_lanes(kb_ref[r]) - qb)
            logit = jnp.where(
                wide_lanes(kp_ref[r]) == qp, s * (inv_root * LOG2E) - gap, MASK_FILL
            )
            t_buf[t * BLK : (t + 1) * BLK] = logit
            top = jnp.maximum(top, fold(logit, jnp.max))
        top = jnp.max(top, axis=0, keepdims=True)
        total = jnp.zeros((8, QB), F32)
        dot = jnp.zeros((8, QB), F32)
        for t in range(tiles):
            here = slice(t * BLK, (t + 1) * BLK)
            e = jnp.exp2(t_buf[here] - top)
            t_buf[here] = e
            total += fold(e, jnp.sum)
            dot += fold(e * d_buf[here], jnp.sum)
        inv = 1.0 / jnp.sum(total, axis=0, keepdims=True)
        delta = jnp.sum(dot, axis=0, keepdims=True) * inv
        sa = jnp.zeros((8, QB), F32)
        sb = jnp.zeros((8, QB), F32)
        for t in range(tiles):
            here = slice(t * BLK, (t + 1) * BLK)
            r = rows(t)
            p = t_buf[here] * inv
            ds = p * (d_buf[here] - delta)
            p_b = p.astype(BF)
            ds_b = ds.astype(BF)
            ds_buf[here] = ds_b
            sa += fold(ds * jnp.abs(wide_lanes(ka_ref[r]) - qa), jnp.sum)
            sb += fold(ds * jnp.abs(wide_lanes(kb_ref[r]) - qb), jnp.sum)
            dv_acc[r] += jnp.dot(p_b, g, preferred_element_type=F32)
            dk_acc[r] += jnp.dot(ds_b, q, preferred_element_type=F32)
        w = pl.ds(pl.multiple_of(start, BLK), tiles * BLK)
        dq = lax.dot_general(
            ds_buf[: tiles * BLK], k_buf[w], tn, preferred_element_type=F32
        )
        dq = (dq * inv_root).astype(BF)
        for i in range(per):
            out_ref[per * b + i, 0] = dq[i * BLK : (i + 1) * BLK]
        for row, v in ((0, sa), (1, sb)):
            v = jnp.sum(v, axis=0, keepdims=True)
            slope_ref[row : row + 1] += sum(v[:, i * BLK : (i + 1) * BLK] for i in range(per))

    def step(b, _):
        wide = win_ref[1, b]

        @pl.when(wide == 0)
        def _():
            work(b, win_ref[0, b] * BLK, NARROW)

        @pl.when(wide != 0)
        def _():
            work(b, 0, TASKS)

        return 0

    lax.fori_loop(0, blocks, step, 0)
    for s in range(TASKS):
        here = slice(s * BLK, (s + 1) * BLK)
        out_ref[s, 1] = (dk_acc[here] * inv_root).astype(BF)
        out_ref[s, 2] = dv_acc[here].astype(BF)


def local(
    self_queries, self_keys, self_values, self_cotangent,
    text_queries, memory_keys, memory_values, text_cotangent,
    slopes, page_counts, page_cols, text_page,
):
    patches = TASKS * BLK
    sds = jax.ShapeDtypeStruct
    task = lax.axis_index("seq")
    is_text = task < TEXT_TASKS

    counts, widths = page_counts[0], page_cols[0]
    ends = [counts[0]]
    for i in range(1, 4):
        ends.append(ends[-1] + counts[i])
    starts = [jnp.int32(0)] + ends[:-1]

    def by_page(ids, per_page):
        out = jnp.broadcast_to(per_page[3], ids.shape)
        for i in (2, 1, 0):
            out = jnp.where(ids == i, per_page[i], out)
        return out

    def layout(pos):
        ids = sum((pos >= e).astype(jnp.int32) for e in ends[:3])
        width = by_page(ids, [widths[i] for i in range(4)])
        off = pos - by_page(ids, starts)
        row = off // width
        return ids, row.astype(F32), (off - row * width).astype(F32)

    own = jnp.clip(task - TEXT_TASKS, 0, HEADS - 1)
    slope = jnp.where(is_text, 0.0, lax.dynamic_slice_in_dim(slopes, own, 1, 1)[:, 0])
    sa, sb = slope[0] * LOG2E, slope[1] * LOG2E
    key_id, key_row, key_col = layout(
        lax.broadcasted_iota(jnp.int32, (patches, BLK), 0)
    )
    pos_id, pos_row, pos_col = layout(jnp.arange(patches, dtype=jnp.int32))
    halves = text_page[0].reshape(TASKS, 2, BLK)
    text_id = lax.dynamic_index_in_dim(halves, task % 2, 1, keepdims=False).reshape(-1)
    q_id = jnp.where(is_text, text_id, pos_id)
    q_info = jnp.stack([pos_row * sa, pos_col * sb, q_id.astype(F32)])
    q_info = jnp.concatenate([q_info, jnp.zeros((5, patches), F32)])
    blocks = q_id.reshape(-1, QB)
    low = jnp.minimum(by_page(blocks[:, 0], starts) // BLK, TASKS - NARROW)
    wide = by_page(blocks[:, -1], ends) > (low + NARROW) * BLK
    window = jnp.stack([low, wide.astype(jnp.int32)])

    by_head = vmem_call(pack_self, sds((4, HEADS, 4, 32, HS), BF))(
        self_queries, self_keys, self_values, self_cotangent
    )
    by_head = lax.all_to_all(by_head, "head", split_axis=0, concat_axis=0, tiled=True)
    sent = vmem_call(pack_tasks, sds((TASKS, 4, BLK, HS), BF))(
        text_queries, memory_keys, memory_values, text_cotangent, by_head
    )
    held = lax.all_to_all(sent, "seq", split_axis=0, concat_axis=0, tiled=True)

    vm = pl.BlockSpec(memory_space=pltpu.VMEM)
    back, slope_part = vmem_call(
        attend,
        (sds((TASKS, 3, BLK, HS), BF), sds((8, BLK), F32)),
        in_specs=[pl.BlockSpec(memory_space=pltpu.SMEM)] + [vm] * 5,
        scratch_shapes=[
            pltpu.VMEM((patches, HS), BF),
            pltpu.VMEM((patches, HS), BF),
            pltpu.VMEM((patches, QB), F32),
            pltpu.VMEM((patches, QB), F32),
            pltpu.VMEM((patches, QB), BF),
            pltpu.VMEM((patches, HS), F32),
            pltpu.VMEM((patches, HS), F32),
        ],
    )(window, key_row * sa, key_col * sb, key_id.astype(F32), q_info, held)

    slope_sum = jnp.sum(slope_part[:2], axis=1) / jnp.where(
        is_text, 1.0, slope * LOG2E
    )
    slope_all = lax.all_gather(slope_sum, ("seq", "dp"), axis=0)
    slope_all = slope_all.reshape(TASKS, -1, 2)[TEXT_TASKS : TEXT_TASKS + HEADS]
    slope_grad = -jnp.sum(slope_all, axis=1).T / patches

    back = lax.all_to_all(back, "seq", split_axis=0, concat_axis=0, tiled=True)
    text_dq, mem_dk, mem_dv, self_out = vmem_call(
        unpack_tasks,
        (
            sds(text_queries.shape, BF),
            sds(memory_keys.shape, BF),
            sds(memory_values.shape, BF),
            sds((4, HEADS, 3, 32, HS), BF),
        ),
    )(back)
    self_out = lax.all_to_all(self_out, "head", split_axis=0, concat_axis=0, tiled=True)
    shape = sds(self_queries.shape, BF)
    self_dq, self_dk, self_dv = vmem_call(unpack_self, (shape, shape, shape))(self_out)
    return self_dq, self_dk, self_dv, slope_grad, text_dq, mem_dk, mem_dv


def solution(mesh):
    rows = P("dp", ("seq", "head"), None)
    cols = P("dp", "seq", "head")
    in_specs = (rows,) * 4 + (cols,) * 4 + (P(None, "head"),) + (P("dp", None),) * 3
    out_specs = (rows,) * 3 + (P(None, "head"),) + (cols,) * 3
    return jax.shard_map(local, mesh=mesh, in_specs=in_specs, out_specs=out_specs, check_vma=False)
```

```python
import functools
import jax
import jax.numpy as jnp
from jax import lax
from jax.experimental import pallas as pl
from jax.experimental.pallas import tpu as pltpu
from jax.sharding import PartitionSpec as P

MASK_FILL = -1e30
LOG2E = 1.4426950408889634
BF = jnp.bfloat16
F32 = jnp.float32

HEADS = 5
TEXT_TASKS = 10
TASKS = 16
BLK = 128
HS = 128
QB = 256
NARROW = 9


def vmem_call(body, out_shapes, **kw):
    return pl.pallas_call(
        body,
        out_shape=out_shapes,
        compiler_params=pltpu.CompilerParams(vmem_limit_bytes=48 * 2**20),
        **kw,
    )


def pack_self(q_ref, k_ref, v_ref, g_ref, out_ref):
    for a, ref in enumerate((q_ref, k_ref, v_ref, g_ref)):
        for x in range(4):
            for h in range(HEADS):
                c = (x * HEADS + h) * HS
                out_ref[x, h, a] = ref[0, :, c : c + HS]


def pack_tasks(tq_ref, mk_ref, mv_ref, tg_ref, self_ref, out_ref):
    for h in range(HEADS):
        cols = slice(h * HS, (h + 1) * HS)
        for j in range(2):
            t = 2 * h + j
            rows = slice(j * BLK, (j + 1) * BLK)
            out_ref[t, 0] = tq_ref[0, rows, cols]
            out_ref[t, 1] = mk_ref[0, :, cols]
            out_ref[t, 2] = mv_ref[0, :, cols]
            out_ref[t, 3] = tg_ref[0, rows, cols]
        for a in range(4):
            for x in range(4):
                out_ref[TEXT_TASKS + h, a, x * 32 : (x + 1) * 32] = self_ref[x, h, a]
    out_ref[TASKS - 1] = jnp.zeros((4, BLK, HS), BF)


def unpack_tasks(in_ref, tq_ref, mk_ref, mv_ref, self_ref):
    for h in range(HEADS):
        cols = slice(h * HS, (h + 1) * HS)
        for j in range(2):
            tq_ref[0, j * BLK : (j + 1) * BLK, cols] = in_ref[2 * h + j, 0]
        mk = in_ref[2 * h, 1].astype(F32) + in_ref[2 * h + 1, 1].astype(F32)
        mv = in_ref[2 * h, 2].astype(F32) + in_ref[2 * h + 1, 2].astype(F32)
        mk_ref[0, :, cols] = mk.astype(BF)
        mv_ref[0, :, cols] = mv.astype(BF)
        for a in range(3):
            for x in range(4):
                self_ref[x, h, a] = in_ref[TEXT_TASKS + h, a, x * 32 : (x + 1) * 32]


def unpack_self(in_ref, q_ref, k_ref, v_ref):
    for a, ref in enumerate((q_ref, k_ref, v_ref)):
        for x in range(4):
            for h in range(HEADS):
                c = (x * HEADS + h) * HS
                ref[0, :, c : c + HS] = in_ref[x, h, a]


def attend(
    win_ref, ka_ref, kb_ref, kp_ref, qi_ref, in_ref, out_ref, slope_ref,
    k_buf, v_buf, t_buf, d_buf, ds_buf, dk_acc, dv_acc,
):
    inv_root = HS ** (-0.5)
    blocks = TASKS * BLK // QB
    per = QB // BLK
    for s in range(TASKS):
        k_buf[s * BLK : (s + 1) * BLK] = in_ref[s, 1]
        v_buf[s * BLK : (s + 1) * BLK] = in_ref[s, 2]
    dk_acc[...] = jnp.zeros_like(dk_acc)
    dv_acc[...] = jnp.zeros_like(dv_acc)
    slope_ref[...] = jnp.zeros_like(slope_ref)
    nt = (((1,), (1,)), ((), ()))
    tn = (((0,), (0,)), ((), ()))

    def wide_lanes(tile):
        return jnp.concatenate([tile] * per, axis=1)

    def fold(x, op):
        return op(x.reshape(BLK // 8, 8, QB), axis=0)

    def work(b, start, tiles):
        q = jnp.concatenate([in_ref[per * b + i, 0] for i in range(per)], axis=0)
        g = jnp.concatenate([in_ref[per * b + i, 3] for i in range(per)], axis=0)
        at = pl.ds(pl.multiple_of(b * QB, QB), QB)
        qa, qb, qp = (qi_ref[i : i + 1, at] for i in range(3))

        def rows(t):
            return pl.ds(pl.multiple_of(start + t * BLK, BLK), BLK)

        top = jnp.full((8, QB), -jnp.inf, F32)
        for t in range(tiles):
            r = rows(t)
            s = lax.dot_general(k_buf[r], q, nt, preferred_element_type=F32)
            d_buf[t * BLK : (t + 1) * BLK] = lax.dot_general(
                v_buf[r], g, nt, preferred_element_type=F32
            )
            gap = jnp.abs(wide_lanes(ka_ref[r]) - qa) + jnp.abs(wide_lanes(kb_ref[r]) - qb)
            logit = jnp.where(
                wide_lanes(kp_ref[r]) == qp, s * (inv_root * LOG2E) - gap, MASK_FILL
            )
            t_buf[t * BLK : (t + 1) * BLK] = logit
            top = jnp.maximum(top, fold(logit, jnp.max))
        top = jnp.max(top, axis=0, keepdims=True)
        total = jnp.zeros((8, QB), F32)
        dot = jnp.zeros((8, QB), F32)
        for t in range(tiles):
            here = slice(t * BLK, (t + 1) * BLK)
            e = jnp.exp2(t_buf[here] - top)
            t_buf[here] = e
            total += fold(e, jnp.sum)
            dot += fold(e * d_buf[here], jnp.sum)
        inv = 1.0 / jnp.sum(total, axis=0, keepdims=True)
        delta = jnp.sum(dot, axis=0, keepdims=True) * inv
        sa = jnp.zeros((8, QB), F32)
        sb = jnp.zeros((8, QB), F32)
        for t in range(tiles):
            here = slice(t * BLK, (t + 1) * BLK)
            r = rows(t)
            p = t_buf[here] * inv
            ds = p * (d_buf[here] - delta)
            p_b = p.astype(BF)
            ds_b = ds.astype(BF)
            ds_buf[here] = ds_b
            sa += fold(ds * jnp.abs(wide_lanes(ka_ref[r]) - qa), jnp.sum)
            sb += fold(ds * jnp.abs(wide_lanes(kb_ref[r]) - qb), jnp.sum)
            dv_acc[r] += jnp.dot(p_b, g, preferred_element_type=F32)
            dk_acc[r] += jnp.dot(ds_b, q, preferred_element_type=F32)
        w = pl.ds(pl.multiple_of(start, BLK), tiles * BLK)
        dq = lax.dot_general(
            ds_buf[: tiles * BLK], k_buf[w], tn, preferred_element_type=F32
        )
        dq = (dq * inv_root).astype(BF)
        for i in range(per):
            out_ref[per * b + i, 0] = dq[i * BLK : (i + 1) * BLK]
        for row, v in ((0, sa), (1, sb)):
            v = jnp.sum(v, axis=0, keepdims=True)
            slope_ref[row : row + 1] += sum(v[:, i * BLK : (i + 1) * BLK] for i in range(per))

    def step(b, _):
        wide = win_ref[1, b]

        @pl.when(wide == 0)
        def _():
            work(b, win_ref[0, b] * BLK, NARROW)

        @pl.when(wide != 0)
        def _():
            work(b, 0, TASKS)

        return 0

    lax.fori_loop(0, blocks, step, 0)
    for s in range(TASKS):
        here = slice(s * BLK, (s + 1) * BLK)
        out_ref[s, 1] = (dk_acc[here] * inv_root).astype(BF)
        out_ref[s, 2] = dv_acc[here].astype(BF)


def local(
    self_queries, self_keys, self_values, self_cotangent,
    text_queries, memory_keys, memory_values, text_cotangent,
    slopes, page_counts, page_cols, text_page,
):
    patches = TASKS * BLK
    sds = jax.ShapeDtypeStruct
    task = lax.axis_index("seq")
    is_text = task < TEXT_TASKS

    counts, widths = page_counts[0], page_cols[0]
    ends = [counts[0]]
    for i in range(1, 4):
        ends.append(ends[-1] + counts[i])
    starts = [jnp.int32(0)] + ends[:-1]

    def by_page(ids, per_page):
        out = jnp.broadcast_to(per_page[3], ids.shape)
        for i in (2, 1, 0):
            out = jnp.where(ids == i, per_page[i], out)
        return out

    def layout(pos):
        ids = sum((pos >= e).astype(jnp.int32) for e in ends[:3])
        width = by_page(ids, [widths[i] for i in range(4)])
        off = pos - by_page(ids, starts)
        row = off // width
        return ids, row.astype(F32), (off - row * width).astype(F32)

    own = jnp.clip(task - TEXT_TASKS, 0, HEADS - 1)
    slope = jnp.where(is_text, 0.0, lax.dynamic_slice_in_dim(slopes, own, 1, 1)[:, 0])
    sa, sb = slope[0] * LOG2E, slope[1] * LOG2E
    key_id, key_row, key_col = layout(
        lax.broadcasted_iota(jnp.int32, (patches, BLK), 0)
    )
    pos_id, pos_row, pos_col = layout(jnp.arange(patches, dtype=jnp.int32))
    halves = text_page[0].reshape(TASKS, 2, BLK)
    text_id = lax.dynamic_index_in_dim(halves, task % 2, 1, keepdims=False).reshape(-1)
    q_id = jnp.where(is_text, text_id, pos_id)
    q_info = jnp.stack([pos_row * sa, pos_col * sb, q_id.astype(F32)])
    q_info = jnp.concatenate([q_info, jnp.zeros((5, patches), F32)])
    blocks = q_id.reshape(-1, QB)
    low = jnp.minimum(by_page(blocks[:, 0], starts) // BLK, TASKS - NARROW)
    wide = by_page(blocks[:, -1], ends) > (low + NARROW) * BLK
    window = jnp.stack([low, wide.astype(jnp.int32)])

    by_head = vmem_call(pack_self, sds((4, HEADS, 4, 32, HS), BF))(
        self_queries, self_keys, self_values, self_cotangent
    )
    by_head = lax.all_to_all(by_head, "head", split_axis=0, concat_axis=0, tiled=True)
    sent = vmem_call(pack_tasks, sds((TASKS, 4, BLK, HS), BF))(
        text_queries, memory_keys, memory_values, text_cotangent, by_head
    )
    held = lax.all_to_all(sent, "seq", split_axis=0, concat_axis=0, tiled=True)

    vm = pl.BlockSpec(memory_space=pltpu.VMEM)
    back, slope_part = vmem_call(
        attend,
        (sds((TASKS, 3, BLK, HS), BF), sds((8, BLK), F32)),
        in_specs=[pl.BlockSpec(memory_space=pltpu.SMEM)] + [vm] * 5,
        scratch_shapes=[
            pltpu.VMEM((patches, HS), BF),
            pltpu.VMEM((patches, HS), BF),
            pltpu.VMEM((patches, QB), F32),
            pltpu.VMEM((patches, QB), F32),
            pltpu.VMEM((patches, QB), BF),
            pltpu.VMEM((patches, HS), F32),
            pltpu.VMEM((patches, HS), F32),
        ],
    )(window, key_row * sa, key_col * sb, key_id.astype(F32), q_info, held)

    slope_sum = jnp.sum(slope_part[:2], axis=1) / jnp.where(
        is_text, 1.0, slope * LOG2E
    )
    mine = jnp.arange(HEADS) == task - TEXT_TASKS
    slope_all = jnp.where(mine[None, :], slope_sum[:, None], 0.0)
    for axis, size in (("dp", 4), ("seq", TASKS)):
        gap = 1
        while gap < size:
            swap = [(i, i ^ gap) for i in range(size)]
            slope_all = slope_all + lax.ppermute(slope_all, axis, swap)
            gap *= 2
    slope_grad = slope_all * (-1.0 / patches)

    back = lax.all_to_all(back, "seq", split_axis=0, concat_axis=0, tiled=True)
    back, slope_grad = lax.optimization_barrier((back, slope_grad))
    text_dq, mem_dk, mem_dv, self_out = vmem_call(
        unpack_tasks,
        (
            sds(text_queries.shape, BF),
            sds(memory_keys.shape, BF),
            sds(memory_values.shape, BF),
            sds((4, HEADS, 3, 32, HS), BF),
        ),
    )(back)
    self_out = lax.all_to_all(self_out, "head", split_axis=0, concat_axis=0, tiled=True)
    shape = sds(self_queries.shape, BF)
    self_dq, self_dk, self_dv = vmem_call(unpack_self, (shape, shape, shape))(self_out)
    return self_dq, self_dk, self_dv, slope_grad, text_dq, mem_dk, mem_dv


def solution(mesh):
    rows = P("dp", ("seq", "head"), None)
    cols = P("dp", "seq", "head")
    in_specs = (rows,) * 4 + (cols,) * 4 + (P(None, "head"),) + (P("dp", None),) * 3
    out_specs = (rows,) * 3 + (P(None, "head"),) + (cols,) * 3
    return jax.shard_map(local, mesh=mesh, in_specs=in_specs, out_specs=out_specs, check_vma=False)
```

```python
import functools
import jax
import jax.numpy as jnp
from jax import lax
from jax.experimental import pallas as pl
from jax.experimental.pallas import tpu as pltpu
from jax.sharding import PartitionSpec as P

MASK_FILL = -1e30
LOG2E = 1.4426950408889634
BF = jnp.bfloat16
F32 = jnp.float32

HEADS = 5
TEXT_TASKS = 10
TASKS = 16
BLK = 128
HS = 128
QB = 256
NARROW = 9


def vmem_call(body, out_shapes, **kw):
    return pl.pallas_call(
        body,
        out_shape=out_shapes,
        compiler_params=pltpu.CompilerParams(vmem_limit_bytes=48 * 2**20),
        **kw,
    )


def pack_self(q_ref, k_ref, v_ref, g_ref, out_ref, sems):
    copies = []
    width = HEADS * HS
    for a, ref in enumerate((q_ref, k_ref, v_ref, g_ref)):
        for x in range(4):
            part = ref.at[0, :, pl.ds(x * width, width)]
            copies.append(pltpu.make_async_copy(part, out_ref.at[x, a], sems.at[a, x]))
            copies[-1].start()
    for copy in copies:
        copy.wait()


def pack_tasks(tq_ref, mk_ref, mv_ref, tg_ref, self_ref, out_ref):
    for h in range(HEADS):
        cols = slice(h * HS, (h + 1) * HS)
        for j in range(2):
            t = 2 * h + j
            rows = slice(j * BLK, (j + 1) * BLK)
            out_ref[t, 0] = tq_ref[0, rows, cols]
            out_ref[t, 1] = mk_ref[0, :, cols]
            out_ref[t, 2] = mv_ref[0, :, cols]
            out_ref[t, 3] = tg_ref[0, rows, cols]
        for a in range(4):
            for x in range(4):
                out_ref[TEXT_TASKS + h, a, x * 32 : (x + 1) * 32] = self_ref[x, a, :, cols]
    out_ref[TASKS - 1] = jnp.zeros((4, BLK, HS), BF)


def unpack_tasks(in_ref, tq_ref, mk_ref, mv_ref, self_ref):
    for h in range(HEADS):
        cols = slice(h * HS, (h + 1) * HS)
        for j in range(2):
            tq_ref[0, j * BLK : (j + 1) * BLK, cols] = in_ref[2 * h + j, 0]
        mk = in_ref[2 * h, 1].astype(F32) + in_ref[2 * h + 1, 1].astype(F32)
        mv = in_ref[2 * h, 2].astype(F32) + in_ref[2 * h + 1, 2].astype(F32)
        mk_ref[0, :, cols] = mk.astype(BF)
        mv_ref[0, :, cols] = mv.astype(BF)
        for a in range(3):
            for x in range(4):
                self_ref[x, h, a] = in_ref[TEXT_TASKS + h, a, x * 32 : (x + 1) * 32]


def unpack_self(in_ref, q_ref, k_ref, v_ref):
    for a, ref in enumerate((q_ref, k_ref, v_ref)):
        for x in range(4):
            for h in range(HEADS):
                c = (x * HEADS + h) * HS
                ref[0, :, c : c + HS] = in_ref[x, h, a]


def attend(
    win_ref, ka_ref, kb_ref, kp_ref, qi_ref, in_ref, out_ref, slope_ref,
    k_buf, v_buf, kt_buf, t_buf, d_buf, ds_buf, dk_acc, dv_acc,
):
    inv_root = HS ** (-0.5)
    blocks = TASKS * BLK // QB
    per = QB // BLK
    for s in range(TASKS):
        k_buf[s * BLK : (s + 1) * BLK] = in_ref[s, 1]
        v_buf[s * BLK : (s + 1) * BLK] = in_ref[s, 2]
        kt_buf[s] = in_ref[s, 1].astype(F32).T.astype(BF)
    dk_acc[...] = jnp.zeros_like(dk_acc)
    dv_acc[...] = jnp.zeros_like(dv_acc)
    slope_ref[...] = jnp.zeros_like(slope_ref)
    nt = (((1,), (1,)), ((), ()))
    tn = (((0,), (0,)), ((), ()))

    def wide_lanes(tile):
        return jnp.concatenate([tile] * per, axis=1)

    def fold(x, op):
        return op(x.reshape(BLK // 8, 8, QB), axis=0)

    def work(b, first, tiles):
        start = first * BLK
        q = jnp.concatenate([in_ref[per * b + i, 0] for i in range(per)], axis=0)
        g = jnp.concatenate([in_ref[per * b + i, 3] for i in range(per)], axis=0)
        at = pl.ds(pl.multiple_of(b * QB, QB), QB)
        qa, qb, qp = (qi_ref[i : i + 1, at] for i in range(3))

        def rows(t):
            return pl.ds(pl.multiple_of(start + t * BLK, BLK), BLK)

        top = jnp.full((8, QB), -jnp.inf, F32)
        for t in range(tiles):
            r = rows(t)
            s = lax.dot_general(k_buf[r], q, nt, preferred_element_type=F32)
            d_buf[t * BLK : (t + 1) * BLK] = lax.dot_general(
                v_buf[r], g, nt, preferred_element_type=F32
            )
            gap = jnp.abs(wide_lanes(ka_ref[r]) - qa) + jnp.abs(wide_lanes(kb_ref[r]) - qb)
            logit = jnp.where(
                wide_lanes(kp_ref[r]) == qp, s * (inv_root * LOG2E) - gap, MASK_FILL
            )
            t_buf[t * BLK : (t + 1) * BLK] = logit
            top = jnp.maximum(top, fold(logit, jnp.max))
        top = jnp.max(top, axis=0, keepdims=True)
        total = jnp.zeros((8, QB), F32)
        dot = jnp.zeros((8, QB), F32)
        for t in range(tiles):
            here = slice(t * BLK, (t + 1) * BLK)
            e = jnp.exp2(t_buf[here] - top)
            total += fold(e, jnp.sum)
            dot += fold(e * d_buf[here], jnp.sum)
        total = jnp.sum(total, axis=0, keepdims=True)
        inv = 1.0 / total
        norm = top + jnp.log2(total)
        delta = jnp.sum(dot, axis=0, keepdims=True) * inv
        sa = jnp.zeros((8, QB), F32)
        sb = jnp.zeros((8, QB), F32)
        for t in range(tiles):
            here = slice(t * BLK, (t + 1) * BLK)
            r = rows(t)
            p = jnp.exp2(t_buf[here] - norm)
            ds = p * (d_buf[here] - delta)
            p_b = p.astype(BF)
            ds_b = ds.astype(BF)
            ds_buf[here] = ds_b
            sa += fold(ds * jnp.abs(wide_lanes(ka_ref[r]) - qa), jnp.sum)
            sb += fold(ds * jnp.abs(wide_lanes(kb_ref[r]) - qb), jnp.sum)
            dv_acc[r] += jnp.dot(p_b, g, preferred_element_type=F32)
            dk_acc[r] += jnp.dot(ds_b, q, preferred_element_type=F32)
        kt = jnp.concatenate([kt_buf[first + t] for t in range(tiles)], axis=1)
        dq = jnp.dot(kt, ds_buf[: tiles * BLK], preferred_element_type=F32).T
        dq = (dq * inv_root).astype(BF)
        for i in range(per):
            out_ref[per * b + i, 0] = dq[i * BLK : (i + 1) * BLK]
        for row, v in ((0, sa), (1, sb)):
            v = jnp.sum(v, axis=0, keepdims=True)
            slope_ref[row : row + 1] += sum(v[:, i * BLK : (i + 1) * BLK] for i in range(per))

    def step(b, _):
        wide = win_ref[1, b]

        @pl.when(wide == 0)
        def _():
            work(b, win_ref[0, b], NARROW)

        @pl.when(wide != 0)
        def _():
            work(b, 0, TASKS)

        return 0

    lax.fori_loop(0, blocks, step, 0)
    for s in range(TASKS):
        here = slice(s * BLK, (s + 1) * BLK)
        out_ref[s, 1] = (dk_acc[here] * inv_root).astype(BF)
        out_ref[s, 2] = dv_acc[here].astype(BF)


def local(
    self_queries, self_keys, self_values, self_cotangent,
    text_queries, memory_keys, memory_values, text_cotangent,
    slopes, page_counts, page_cols, text_page,
):
    patches = TASKS * BLK
    sds = jax.ShapeDtypeStruct
    task = lax.axis_index("seq")
    is_text = task < TEXT_TASKS

    counts, widths = page_counts[0], page_cols[0]
    ends = [counts[0]]
    for i in range(1, 4):
        ends.append(ends[-1] + counts[i])
    starts = [jnp.int32(0)] + ends[:-1]

    def by_page(ids, per_page):
        out = jnp.broadcast_to(per_page[3], ids.shape)
        for i in (2, 1, 0):
            out = jnp.where(ids == i, per_page[i], out)
        return out

    def layout(pos):
        ids = sum((pos >= e).astype(jnp.int32) for e in ends[:3])
        width = by_page(ids, [widths[i] for i in range(4)])
        off = pos - by_page(ids, starts)
        row = off // width
        return ids, row.astype(F32), (off - row * width).astype(F32)

    own = jnp.clip(task - TEXT_TASKS, 0, HEADS - 1)
    slope = jnp.where(is_text, 0.0, lax.dynamic_slice_in_dim(slopes, own, 1, 1)[:, 0])
    sa, sb = slope[0] * LOG2E, slope[1] * LOG2E
    key_id, key_row, key_col = layout(
        lax.broadcasted_iota(jnp.int32, (patches, BLK), 0)
    )
    pos_id, pos_row, pos_col = layout(jnp.arange(patches, dtype=jnp.int32))
    halves = text_page[0].reshape(TASKS, 2, BLK)
    text_id = lax.dynamic_index_in_dim(halves, task % 2, 1, keepdims=False).reshape(-1)
    q_id = jnp.where(is_text, text_id, pos_id)
    q_info = jnp.stack([pos_row * sa, pos_col * sb, q_id.astype(F32)])
    q_info = jnp.concatenate([q_info, jnp.zeros((5, patches), F32)])
    blocks = q_id.reshape(-1, QB)
    low = jnp.minimum(by_page(blocks[:, 0], starts) // BLK, TASKS - NARROW)
    wide = by_page(blocks[:, -1], ends) > (low + NARROW) * BLK
    window = jnp.stack([low, wide.astype(jnp.int32)])

    hbm = pl.BlockSpec(memory_space=pltpu.HBM)
    by_head = pl.pallas_call(
        pack_self,
        out_shape=sds((4, 4, 32, HEADS * HS), BF),
        in_specs=[hbm] * 4,
        out_specs=hbm,
        scratch_shapes=[pltpu.SemaphoreType.DMA((4, 4))],
    )(self_queries, self_keys, self_values, self_cotangent)
    by_head = lax.all_to_all(by_head, "head", split_axis=0, concat_axis=0, tiled=True)
    sent = vmem_call(pack_tasks, sds((TASKS, 4, BLK, HS), BF))(
        text_queries, memory_keys, memory_values, text_cotangent, by_head
    )
    held = lax.all_to_all(sent, "seq", split_axis=0, concat_axis=0, tiled=True)

    vm = pl.BlockSpec(memory_space=pltpu.VMEM)
    back, slope_part = vmem_call(
        attend,
        (sds((TASKS, 3, BLK, HS), BF), sds((8, BLK), F32)),
        in_specs=[pl.BlockSpec(memory_space=pltpu.SMEM)] + [vm] * 5,
        scratch_shapes=[
            pltpu.VMEM((patches, HS), BF),
            pltpu.VMEM((patches, HS), BF),
            pltpu.VMEM((TASKS, HS, BLK), BF),
            pltpu.VMEM((patches, QB), F32),
            pltpu.VMEM((patches, QB), F32),
            pltpu.VMEM((patches, QB), BF),
            pltpu.VMEM((patches, HS), F32),
            pltpu.VMEM((patches, HS), F32),
        ],
    )(window, key_row * sa, key_col * sb, key_id.astype(F32), q_info, held)

    slope_sum = jnp.sum(slope_part[:2], axis=1) / jnp.where(
        is_text, 1.0, slope * LOG2E
    )
    mine = jnp.arange(HEADS) == task - TEXT_TASKS
    slope_all = jnp.where(mine[None, :], slope_sum[:, None], 0.0)
    def add_over(total, axis, size, gaps):
        for gap in gaps:
            swap = [(i, i ^ gap) for i in range(size)]
            total = total + lax.ppermute(total, axis, swap)
        return total

    slope_all = add_over(slope_all, "dp", 4, (1, 2))
    slope_all = add_over(slope_all, "seq", TASKS, (1,))
    back = lax.all_to_all(back, "seq", split_axis=0, concat_axis=0, tiled=True)
    back, slope_all = lax.optimization_barrier((back, slope_all))
    slope_grad = add_over(slope_all, "seq", TASKS, (2, 4, 8)) * (-1.0 / patches)

    text_dq, mem_dk, mem_dv, self_out = vmem_call(
        unpack_tasks,
        (
            sds(text_queries.shape, BF),
            sds(memory_keys.shape, BF),
            sds(memory_values.shape, BF),
            sds((4, HEADS, 3, 32, HS), BF),
        ),
    )(back)
    self_out = lax.all_to_all(self_out, "head", split_axis=0, concat_axis=0, tiled=True)
    shape = sds(self_queries.shape, BF)
    self_dq, self_dk, self_dv = vmem_call(unpack_self, (shape, shape, shape))(self_out)
    return self_dq, self_dk, self_dv, slope_grad, text_dq, mem_dk, mem_dv


def solution(mesh):
    rows = P("dp", ("seq", "head"), None)
    cols = P("dp", "seq", "head")
    in_specs = (rows,) * 4 + (cols,) * 4 + (P(None, "head"),) + (P("dp", None),) * 3
    out_specs = (rows,) * 3 + (P(None, "head"),) + (cols,) * 3
    return jax.shard_map(local, mesh=mesh, in_specs=in_specs, out_specs=out_specs, check_vma=False)
```

```python
import functools
import jax
import jax.numpy as jnp
from jax import lax
from jax.experimental import pallas as pl
from jax.experimental.pallas import tpu as pltpu
from jax.sharding import PartitionSpec as P

MASK_FILL = -1e30
LOG2E = 1.4426950408889634
BF = jnp.bfloat16
F32 = jnp.float32

HEADS = 5
TEXT_TASKS = 10
TASKS = 16
BLK = 128
HS = 128
QB = 256
NARROW = 9


def vmem_call(body, out_shapes, **kw):
    return pl.pallas_call(
        body,
        out_shape=out_shapes,
        compiler_params=pltpu.CompilerParams(vmem_limit_bytes=48 * 2**20),
        **kw,
    )


def pack_self(q_ref, k_ref, v_ref, g_ref, *refs):
    outs, sems = refs[:4], refs[4]
    me = lax.axis_index("head")
    width = HEADS * HS
    copies = []
    for gap in (2, 1, 3, 0):
        at = pl.ds(pl.multiple_of((me ^ gap) * width, HS), width)
        for a, ref in enumerate((q_ref, k_ref, v_ref, g_ref)):
            copies.append(
                pltpu.make_async_copy(ref.at[0, :, at], outs[gap].at[a], sems.at[gap, a])
            )
            copies[-1].start()
    for copy in copies:
        copy.wait()


def pack_text(tq_ref, mk_ref, mv_ref, tg_ref, out_ref):
    for h in range(HEADS):
        cols = slice(h * HS, (h + 1) * HS)
        for j in range(2):
            t = 2 * h + j
            rows = slice(j * BLK, (j + 1) * BLK)
            out_ref[t, 0] = tq_ref[0, rows, cols]
            out_ref[t, 1] = mk_ref[0, :, cols]
            out_ref[t, 2] = mv_ref[0, :, cols]
            out_ref[t, 3] = tg_ref[0, rows, cols]
    out_ref[TEXT_TASKS:] = jnp.zeros((TASKS - TEXT_TASKS, 4, BLK, HS), BF)


def pack_heads(s0_ref, s1_ref, s2_ref, s3_ref, text_ref, out_ref, buf, sem):
    me = lax.axis_index("head")
    for h in range(HEADS):
        cols = slice(h * HS, (h + 1) * HS)
        for gap, ref in enumerate((s0_ref, s1_ref, s2_ref, s3_ref)):
            at = pl.ds(pl.multiple_of((me ^ gap) * 32, 32), 32)
            for a in range(4):
                buf[h, a, at] = ref[a, :, cols]
    copy = pltpu.make_async_copy(buf, out_ref.at[pl.ds(TEXT_TASKS, HEADS)], sem)
    copy.start()
    copy.wait()


def unpack_tasks(
    in_ref, tq_ref, mk_ref, mv_ref, slope_ref, s0_ref, s1_ref, s2_ref, s3_ref
):
    me = lax.axis_index("head")
    k, v = (slice(i * BLK, (i + 1) * BLK) for i in (1, 2))
    slope_ref[...] = jnp.zeros_like(slope_ref)
    for h in range(HEADS):
        cols = slice(h * HS, (h + 1) * HS)
        for j in range(2):
            tq_ref[0, j * BLK : (j + 1) * BLK, cols] = in_ref[2 * h + j, :BLK]
        mk = in_ref[2 * h, k].astype(F32) + in_ref[2 * h + 1, k].astype(F32)
        mv = in_ref[2 * h, v].astype(F32) + in_ref[2 * h + 1, v].astype(F32)
        mk_ref[0, :, cols] = mk.astype(BF)
        mv_ref[0, :, cols] = mv.astype(BF)
        for gap, ref in enumerate((s0_ref, s1_ref, s2_ref, s3_ref)):
            for a in range(3):
                at = pl.ds(pl.multiple_of(a * BLK + (me ^ gap) * 32, 32), 32)
                ref[a, :, cols] = in_ref[TEXT_TASKS + h, at]
        pieces = in_ref[TEXT_TASKS + h, 3 * BLK :].astype(F32)
        for i in range(2):
            whole = pieces[3 * i : 3 * i + 1] + pieces[3 * i + 1 : 3 * i + 2]
            slope_ref[i, h : h + 1] = whole + pieces[3 * i + 2 : 3 * i + 3]


def unpack_self(s0_ref, s1_ref, s2_ref, s3_ref, q_ref, k_ref, v_ref):
    me = lax.axis_index("head")
    width = HEADS * HS
    for gap, part in enumerate((s0_ref, s1_ref, s2_ref, s3_ref)):
        at = pl.ds(pl.multiple_of((me ^ gap) * width, HS), width)
        for a, ref in enumerate((q_ref, k_ref, v_ref)):
            ref[0, :, at] = part[a]


def attend(
    win_ref, ka_ref, kb_ref, kp_ref, qi_ref, in_ref, out_ref,
    k_buf, v_buf, kt_buf, t_buf, d_buf, ds_buf, dk_acc, dv_acc, slope_ref,
):
    inv_root = HS ** (-0.5)
    blocks = TASKS * BLK // QB
    per = QB // BLK
    for s in range(TASKS):
        k_buf[s * BLK : (s + 1) * BLK] = in_ref[s, 1]
        v_buf[s * BLK : (s + 1) * BLK] = in_ref[s, 2]
        kt_buf[s] = in_ref[s, 1].astype(F32).T.astype(BF)
    dk_acc[...] = jnp.zeros_like(dk_acc)
    dv_acc[...] = jnp.zeros_like(dv_acc)
    slope_ref[...] = jnp.zeros_like(slope_ref)
    nt = (((1,), (1,)), ((), ()))
    tn = (((0,), (0,)), ((), ()))

    def wide_lanes(tile):
        return jnp.concatenate([tile] * per, axis=1)

    def fold(x, op):
        return op(x.reshape(BLK // 8, 8, QB), axis=0)

    def work(b, first, tiles):
        start = first * BLK
        q = jnp.concatenate([in_ref[per * b + i, 0] for i in range(per)], axis=0)
        g = jnp.concatenate([in_ref[per * b + i, 3] for i in range(per)], axis=0)
        at = pl.ds(pl.multiple_of(b * QB, QB), QB)
        qa, qb, qp = (qi_ref[i : i + 1, at] for i in range(3))

        def rows(t):
            return pl.ds(pl.multiple_of(start + t * BLK, BLK), BLK)

        top = jnp.full((8, QB), -jnp.inf, F32)
        for t in range(tiles):
            r = rows(t)
            s = lax.dot_general(k_buf[r], q, nt, preferred_element_type=F32)
            d_buf[t * BLK : (t + 1) * BLK] = lax.dot_general(
                v_buf[r], g, nt, preferred_element_type=F32
            )
            gap = jnp.abs(wide_lanes(ka_ref[r]) - qa) + jnp.abs(wide_lanes(kb_ref[r]) - qb)
            logit = jnp.where(
                wide_lanes(kp_ref[r]) == qp, s * (inv_root * LOG2E) - gap, MASK_FILL
            )
            t_buf[t * BLK : (t + 1) * BLK] = logit
            top = jnp.maximum(top, fold(logit, jnp.max))
        top = jnp.max(top, axis=0, keepdims=True)
        total = jnp.zeros((8, QB), F32)
        dot = jnp.zeros((8, QB), F32)
        for t in range(tiles):
            here = slice(t * BLK, (t + 1) * BLK)
            e = jnp.exp2(t_buf[here] - top)
            total += fold(e, jnp.sum)
            dot += fold(e * d_buf[here], jnp.sum)
        total = jnp.sum(total, axis=0, keepdims=True)
        inv = 1.0 / total
        norm = top + jnp.log2(total)
        delta = jnp.sum(dot, axis=0, keepdims=True) * inv
        sa = jnp.zeros((8, QB), F32)
        sb = jnp.zeros((8, QB), F32)
        for t in range(tiles):
            here = slice(t * BLK, (t + 1) * BLK)
            r = rows(t)
            p = jnp.exp2(t_buf[here] - norm)
            ds = p * (d_buf[here] - delta)
            p_b = p.astype(BF)
            ds_b = ds.astype(BF)
            ds_buf[here] = ds_b
            sa += fold(ds * jnp.abs(wide_lanes(ka_ref[r]) - qa), jnp.sum)
            sb += fold(ds * jnp.abs(wide_lanes(kb_ref[r]) - qb), jnp.sum)
            dv_acc[r] += jnp.dot(p_b, g, preferred_element_type=F32)
            dk_acc[r] += jnp.dot(ds_b, q, preferred_element_type=F32)
        kt = jnp.concatenate([kt_buf[first + t] for t in range(tiles)], axis=1)
        dq = jnp.dot(kt, ds_buf[: tiles * BLK], preferred_element_type=F32).T
        dq = (dq * inv_root).astype(BF)
        for i in range(per):
            out_ref[per * b + i, :BLK] = dq[i * BLK : (i + 1) * BLK]
        for row, v in ((0, sa), (1, sb)):
            v = jnp.sum(v, axis=0, keepdims=True)
            slope_ref[row : row + 1] += sum(v[:, i * BLK : (i + 1) * BLK] for i in range(per))

    def step(b, _):
        wide = win_ref[1, b]

        @pl.when(wide == 0)
        def _():
            work(b, win_ref[0, b], NARROW)

        @pl.when(wide != 0)
        def _():
            work(b, 0, TASKS)

        return 0

    lax.fori_loop(0, blocks, step, 0)
    line = lax.broadcasted_iota(jnp.int32, (16, BLK), 0)
    pieces = jnp.zeros((16, BLK), F32)
    for row in range(2):
        rest = jnp.broadcast_to(slope_ref[row : row + 1], (16, BLK))
        for i in range(3):
            piece = rest.astype(BF).astype(F32)
            rest = rest - piece
            pieces = jnp.where(line == 3 * row + i, piece, pieces)
    pieces = pieces.astype(BF)
    for s in range(TASKS):
        here = slice(s * BLK, (s + 1) * BLK)
        out_ref[s, BLK : 2 * BLK] = (dk_acc[here] * inv_root).astype(BF)
        out_ref[s, 2 * BLK : 3 * BLK] = dv_acc[here].astype(BF)
        out_ref[s, 3 * BLK :] = pieces


def local(
    self_queries, self_keys, self_values, self_cotangent,
    text_queries, memory_keys, memory_values, text_cotangent,
    slopes, page_counts, page_cols, text_page,
):
    patches = TASKS * BLK
    sds = jax.ShapeDtypeStruct
    task = lax.axis_index("seq")
    is_text = task < TEXT_TASKS

    counts, widths = page_counts[0], page_cols[0]
    ends = [counts[0]]
    for i in range(1, 4):
        ends.append(ends[-1] + counts[i])
    starts = [jnp.int32(0)] + ends[:-1]

    def by_page(ids, per_page):
        out = jnp.broadcast_to(per_page[3], ids.shape)
        for i in (2, 1, 0):
            out = jnp.where(ids == i, per_page[i], out)
        return out

    def layout(pos):
        ids = sum((pos >= e).astype(jnp.int32) for e in ends[:3])
        width = by_page(ids, [widths[i] for i in range(4)])
        off = pos - by_page(ids, starts)
        row = off // width
        return ids, row.astype(F32), (off - row * width).astype(F32)

    own = jnp.clip(task - TEXT_TASKS, 0, HEADS - 1)
    slope = jnp.where(is_text, 0.0, lax.dynamic_slice_in_dim(slopes, own, 1, 1)[:, 0])
    sa, sb = slope[0] * LOG2E, slope[1] * LOG2E
    key_id, key_row, key_col = layout(
        lax.broadcasted_iota(jnp.int32, (patches, BLK), 0)
    )
    pos_id, pos_row, pos_col = layout(jnp.arange(patches, dtype=jnp.int32))
    halves = text_page[0].reshape(TASKS, 2, BLK)
    text_id = lax.dynamic_index_in_dim(halves, task % 2, 1, keepdims=False).reshape(-1)
    q_id = jnp.where(is_text, text_id, pos_id)
    q_info = jnp.stack([pos_row * sa, pos_col * sb, q_id.astype(F32)])
    q_info = jnp.concatenate([q_info, jnp.zeros((5, patches), F32)])
    blocks = q_id.reshape(-1, QB)
    low = jnp.minimum(by_page(blocks[:, 0], starts) // BLK, TASKS - NARROW)
    wide = by_page(blocks[:, -1], ends) > (low + NARROW) * BLK
    window = jnp.stack([low, wide.astype(jnp.int32)])

    def swap_heads(parts):
        own, out = parts[0], [None] * 4
        for gap in (2, 1, 3):
            swap = [(i, i ^ gap) for i in range(4)]
            out[gap] = lax.ppermute(parts[gap], "head", swap)
        return [own] + out[1:]

    hbm = pl.BlockSpec(memory_space=pltpu.HBM)
    by_head = pl.pallas_call(
        pack_self,
        out_shape=[sds((4, 32, HEADS * HS), BF)] * 4,
        in_specs=[hbm] * 4,
        out_specs=[pl.BlockSpec(memory_space=pltpu.VMEM)] * 4,
        scratch_shapes=[pltpu.SemaphoreType.DMA((4, 4))],
    )(self_queries, self_keys, self_values, self_cotangent)
    task_shape = sds((TASKS, 4, BLK, HS), BF)
    vm = pl.BlockSpec(memory_space=pltpu.VMEM)
    sent = vmem_call(pack_text, task_shape)(
        text_queries, memory_keys, memory_values, text_cotangent
    )
    by_head = swap_heads(by_head)
    sent = vmem_call(
        pack_heads,
        task_shape,
        in_specs=[vm] * 4 + [hbm],
        out_specs=hbm,
        scratch_shapes=[pltpu.VMEM((HEADS, 4, BLK, HS), BF), pltpu.SemaphoreType.DMA],
        input_output_aliases={4: 0},
    )(*by_head, sent)
    held = lax.all_to_all(sent, "seq", split_axis=0, concat_axis=0, tiled=True)
    back = vmem_call(
        attend,
        sds((TASKS, 3 * BLK + 16, HS), BF),
        in_specs=[pl.BlockSpec(memory_space=pltpu.SMEM)] + [vm] * 5,
        scratch_shapes=[
            pltpu.VMEM((patches, HS), BF),
            pltpu.VMEM((patches, HS), BF),
            pltpu.VMEM((TASKS, HS, BLK), BF),
            pltpu.VMEM((patches, QB), F32),
            pltpu.VMEM((patches, QB), F32),
            pltpu.VMEM((patches, QB), BF),
            pltpu.VMEM((patches, HS), F32),
            pltpu.VMEM((patches, HS), F32),
            pltpu.VMEM((8, BLK), F32),
        ],
    )(window, key_row * sa, key_col * sb, key_id.astype(F32), q_info, held)

    back = lax.all_to_all(back, "seq", split_axis=0, concat_axis=0, tiled=True)
    part = sds((3, 32, HEADS * HS), BF)
    text_dq, mem_dk, mem_dv, slope_sum, *self_out = vmem_call(
        unpack_tasks,
        (
            sds(text_queries.shape, BF),
            sds(memory_keys.shape, BF),
            sds(memory_values.shape, BF),
            sds((2, 8, BLK), F32),
            *(part,) * 4,
        ),
    )(back)
    self_out = swap_heads(self_out)
    slope_sum, self_out[2] = lax.optimization_barrier((slope_sum, self_out[2]))
    slope_sum = jnp.sum(slope_sum[:, :HEADS], axis=2) / (slopes * (LOG2E * -patches))
    near, far, last = (
        lax.ppermute(slope_sum, "dp", [(i, i ^ gap) for i in range(4)])
        for gap in (1, 2, 3)
    )
    slope_grad = (slope_sum + near) + (far + last)
    shape = sds(self_queries.shape, BF)
    self_dq, self_dk, self_dv = vmem_call(unpack_self, (shape, shape, shape))(*self_out)
    return self_dq, self_dk, self_dv, slope_grad, text_dq, mem_dk, mem_dv


def solution(mesh):
    rows = P("dp", ("seq", "head"), None)
    cols = P("dp", "seq", "head")
    in_specs = (rows,) * 4 + (cols,) * 4 + (P(None, "head"),) + (P("dp", None),) * 3
    out_specs = (rows,) * 3 + (P(None, "head"),) + (cols,) * 3
    return jax.shard_map(local, mesh=mesh, in_specs=in_specs, out_specs=out_specs, check_vma=False)
```

```python
import functools
import jax
import jax.numpy as jnp
from jax import lax
from jax.experimental import pallas as pl
from jax.experimental.pallas import tpu as pltpu
from jax.sharding import PartitionSpec as P

MASK_FILL = -1e30
LOG2E = 1.4426950408889634
BF = jnp.bfloat16
F32 = jnp.float32

HEADS = 5
TEXT_TASKS = 10
TASKS = 16
BLK = 128
HS = 128
QB = 256
SIZES = (6, 9, 12, 16)


def vmem_call(body, out_shapes, **kw):
    return pl.pallas_call(
        body,
        out_shape=out_shapes,
        compiler_params=pltpu.CompilerParams(vmem_limit_bytes=48 * 2**20),
        **kw,
    )


def pack_self(q_ref, k_ref, v_ref, g_ref, *refs):
    outs, sems = refs[:4], refs[4]
    me = lax.axis_index("head")
    width = HEADS * HS
    copies = []
    for gap in (2, 1, 3, 0):
        at = pl.ds(pl.multiple_of((me ^ gap) * width, HS), width)
        for a, ref in enumerate((q_ref, k_ref, v_ref, g_ref)):
            copies.append(
                pltpu.make_async_copy(ref.at[0, :, at], outs[gap].at[a], sems.at[gap, a])
            )
            copies[-1].start()
    for copy in copies:
        copy.wait()


def pack_text(tq_ref, mk_ref, mv_ref, tg_ref, out_ref):
    for h in range(HEADS):
        cols = slice(h * HS, (h + 1) * HS)
        for j in range(2):
            t = 2 * h + j
            rows = slice(j * BLK, (j + 1) * BLK)
            out_ref[t, 0] = tq_ref[0, rows, cols]
            out_ref[t, 1] = mk_ref[0, :, cols]
            out_ref[t, 2] = mv_ref[0, :, cols]
            out_ref[t, 3] = tg_ref[0, rows, cols]
    out_ref[TEXT_TASKS:] = jnp.zeros((TASKS - TEXT_TASKS, 4, BLK, HS), BF)


def pack_heads(s0_ref, s1_ref, s2_ref, s3_ref, text_ref, out_ref, buf, sem):
    me = lax.axis_index("head")
    for h in range(HEADS):
        cols = slice(h * HS, (h + 1) * HS)
        for gap, ref in enumerate((s0_ref, s1_ref, s2_ref, s3_ref)):
            at = pl.ds(pl.multiple_of((me ^ gap) * 32, 32), 32)
            for a in range(4):
                buf[h, a, at] = ref[a, :, cols]
    copy = pltpu.make_async_copy(buf, out_ref.at[pl.ds(TEXT_TASKS, HEADS)], sem)
    copy.start()
    copy.wait()


def unpack_tasks(
    in_ref, tq_ref, mk_ref, mv_ref, slope_ref, s0_ref, s1_ref, s2_ref, s3_ref
):
    me = lax.axis_index("head")
    k, v = (slice(i * BLK, (i + 1) * BLK) for i in (1, 2))
    slope_ref[...] = jnp.zeros_like(slope_ref)
    for h in range(HEADS):
        cols = slice(h * HS, (h + 1) * HS)
        for j in range(2):
            tq_ref[0, j * BLK : (j + 1) * BLK, cols] = in_ref[2 * h + j, :BLK]
        mk = in_ref[2 * h, k].astype(F32) + in_ref[2 * h + 1, k].astype(F32)
        mv = in_ref[2 * h, v].astype(F32) + in_ref[2 * h + 1, v].astype(F32)
        mk_ref[0, :, cols] = mk.astype(BF)
        mv_ref[0, :, cols] = mv.astype(BF)
        for gap, ref in enumerate((s0_ref, s1_ref, s2_ref, s3_ref)):
            for a in range(3):
                at = pl.ds(pl.multiple_of(a * BLK + (me ^ gap) * 32, 32), 32)
                ref[a, :, cols] = in_ref[TEXT_TASKS + h, at]
        pieces = in_ref[TEXT_TASKS + h, 3 * BLK :].astype(F32)
        for i in range(2):
            whole = pieces[3 * i : 3 * i + 1] + pieces[3 * i + 1 : 3 * i + 2]
            slope_ref[i, h : h + 1] = whole + pieces[3 * i + 2 : 3 * i + 3]


def unpack_self(s0_ref, s1_ref, s2_ref, s3_ref, q_ref, k_ref, v_ref):
    me = lax.axis_index("head")
    width = HEADS * HS
    for gap, part in enumerate((s0_ref, s1_ref, s2_ref, s3_ref)):
        at = pl.ds(pl.multiple_of((me ^ gap) * width, HS), width)
        for a, ref in enumerate((q_ref, k_ref, v_ref)):
            ref[0, :, at] = part[a]


def attend(
    win_ref, ka_ref, kb_ref, kp_ref, qi_ref, in_ref, out_ref,
    kt_buf, t_buf, d_buf, ds_buf, dk_acc, dv_acc, slope_ref,
):
    inv_root = HS ** (-0.5)
    blocks = TASKS * BLK // QB
    per = QB // BLK
    for s in range(TASKS):
        kt_buf[s] = in_ref[s, 1].T
    dk_acc[...] = jnp.zeros_like(dk_acc)
    dv_acc[...] = jnp.zeros_like(dv_acc)
    slope_ref[...] = jnp.zeros_like(slope_ref)
    nt = (((1,), (1,)), ((), ()))
    tn = (((0,), (0,)), ((), ()))

    def wide_lanes(tile):
        return jnp.concatenate([tile] * per, axis=1)

    def fold(x, op):
        return op(x.reshape(BLK // 8, 8, QB), axis=0)

    def work(b, first, tiles):
        start = first * BLK
        q = jnp.concatenate([in_ref[per * b + i, 0] for i in range(per)], axis=0)
        g = jnp.concatenate([in_ref[per * b + i, 3] for i in range(per)], axis=0)
        at = pl.ds(pl.multiple_of(b * QB, QB), QB)
        qa, qb, qp = (qi_ref[i : i + 1, at] for i in range(3))

        def rows(t):
            return pl.ds(pl.multiple_of(start + t * BLK, BLK), BLK)

        top = jnp.full((8, QB), -jnp.inf, F32)
        for t in range(tiles):
            r = rows(t)
            s = lax.dot_general(in_ref[first + t, 1], q, nt, preferred_element_type=F32)
            d_buf[t * BLK : (t + 1) * BLK] = lax.dot_general(
                in_ref[first + t, 2], g, nt, preferred_element_type=F32
            )
            gap = jnp.abs(wide_lanes(ka_ref[r]) - qa) + jnp.abs(wide_lanes(kb_ref[r]) - qb)
            logit = jnp.where(
                wide_lanes(kp_ref[r]) == qp, s * (inv_root * LOG2E) - gap, MASK_FILL
            )
            t_buf[t * BLK : (t + 1) * BLK] = logit
            top = jnp.maximum(top, fold(logit, jnp.max))
        top = jnp.max(top, axis=0, keepdims=True)
        total = jnp.zeros((8, QB), F32)
        dot = jnp.zeros((8, QB), F32)
        for t in range(tiles):
            here = slice(t * BLK, (t + 1) * BLK)
            e = jnp.exp2(t_buf[here] - top)
            total += fold(e, jnp.sum)
            dot += fold(e * d_buf[here], jnp.sum)
        total = jnp.sum(total, axis=0, keepdims=True)
        inv = 1.0 / total
        norm = top + jnp.log2(total)
        delta = jnp.sum(dot, axis=0, keepdims=True) * inv
        sa = jnp.zeros((8, QB), F32)
        sb = jnp.zeros((8, QB), F32)
        for t in range(tiles):
            here = slice(t * BLK, (t + 1) * BLK)
            r = rows(t)
            p = jnp.exp2(t_buf[here] - norm)
            ds = p * (d_buf[here] - delta)
            p_b = p.astype(BF)
            ds_b = ds.astype(BF)
            ds_buf[here] = ds_b
            sa += fold(ds * jnp.abs(wide_lanes(ka_ref[r]) - qa), jnp.sum)
            sb += fold(ds * jnp.abs(wide_lanes(kb_ref[r]) - qb), jnp.sum)
            dv_acc[r] += jnp.dot(p_b, g, preferred_element_type=F32)
            dk_acc[r] += jnp.dot(ds_b, q, preferred_element_type=F32)
        kt = jnp.concatenate([kt_buf[first + t] for t in range(tiles)], axis=1)
        dq = jnp.dot(kt, ds_buf[: tiles * BLK], preferred_element_type=F32).T
        dq = (dq * inv_root).astype(BF)
        for i in range(per):
            out_ref[per * b + i, :BLK] = dq[i * BLK : (i + 1) * BLK]
        for row, v in ((0, sa), (1, sb)):
            v = jnp.sum(v, axis=0, keepdims=True)
            slope_ref[row : row + 1] += sum(v[:, i * BLK : (i + 1) * BLK] for i in range(per))

    def step(b, _):
        for kind, tiles in enumerate(SIZES):

            @pl.when(win_ref[1, b] == kind)
            def _(tiles=tiles):
                work(b, win_ref[0, b], tiles)

        return 0

    lax.fori_loop(0, blocks, step, 0)
    line = lax.broadcasted_iota(jnp.int32, (16, BLK), 0)
    pieces = jnp.zeros((16, BLK), F32)
    for row in range(2):
        rest = jnp.broadcast_to(slope_ref[row : row + 1], (16, BLK))
        for i in range(3):
            piece = rest.astype(BF).astype(F32)
            rest = rest - piece
            pieces = jnp.where(line == 3 * row + i, piece, pieces)
    pieces = pieces.astype(BF)
    for s in range(TASKS):
        here = slice(s * BLK, (s + 1) * BLK)
        out_ref[s, BLK : 2 * BLK] = (dk_acc[here] * inv_root).astype(BF)
        out_ref[s, 2 * BLK : 3 * BLK] = dv_acc[here].astype(BF)
        out_ref[s, 3 * BLK :] = pieces


def local(
    self_queries, self_keys, self_values, self_cotangent,
    text_queries, memory_keys, memory_values, text_cotangent,
    slopes, page_counts, page_cols, text_page,
):
    patches = TASKS * BLK
    sds = jax.ShapeDtypeStruct
    task = lax.axis_index("seq")
    is_text = task < TEXT_TASKS

    counts, widths = page_counts[0], page_cols[0]
    ends = [counts[0]]
    for i in range(1, 4):
        ends.append(ends[-1] + counts[i])
    starts = [jnp.int32(0)] + ends[:-1]

    def by_page(ids, per_page):
        out = jnp.broadcast_to(per_page[3], ids.shape)
        for i in (2, 1, 0):
            out = jnp.where(ids == i, per_page[i], out)
        return out

    def layout(pos):
        ids = sum((pos >= e).astype(jnp.int32) for e in ends[:3])
        width = by_page(ids, [widths[i] for i in range(4)])
        off = pos - by_page(ids, starts)
        row = off // width
        return ids, row.astype(F32), (off - row * width).astype(F32)

    own = jnp.clip(task - TEXT_TASKS, 0, HEADS - 1)
    slope = jnp.where(is_text, 0.0, lax.dynamic_slice_in_dim(slopes, own, 1, 1)[:, 0])
    sa, sb = slope[0] * LOG2E, slope[1] * LOG2E
    key_id, key_row, key_col = layout(
        lax.broadcasted_iota(jnp.int32, (patches, BLK), 0)
    )
    pos_id, pos_row, pos_col = layout(jnp.arange(patches, dtype=jnp.int32))
    halves = text_page[0].reshape(TASKS, 2, BLK)
    text_id = lax.dynamic_index_in_dim(halves, task % 2, 1, keepdims=False).reshape(-1)
    q_id = jnp.where(is_text, text_id, pos_id)
    q_info = jnp.stack([pos_row * sa, pos_col * sb, q_id.astype(F32)])
    q_info = jnp.concatenate([q_info, jnp.zeros((5, patches), F32)])
    blocks = q_id.reshape(-1, QB)
    low = by_page(blocks[:, 0], starts) // BLK
    high = (by_page(blocks[:, -1], ends) + BLK - 1) // BLK
    first, kind = jnp.zeros_like(low), jnp.full_like(low, len(SIZES) - 1)
    for i in reversed(range(len(SIZES) - 1)):
        at = jnp.minimum(low, TASKS - SIZES[i])
        fits = high <= at + SIZES[i]
        first, kind = jnp.where(fits, at, first), jnp.where(fits, i, kind)
    window = jnp.stack([first, kind])

    def swap_heads(parts):
        own, out = parts[0], [None] * 4
        for gap in (2, 1, 3):
            swap = [(i, i ^ gap) for i in range(4)]
            out[gap] = lax.ppermute(parts[gap], "head", swap)
        return [own] + out[1:]

    hbm = pl.BlockSpec(memory_space=pltpu.HBM)
    by_head = pl.pallas_call(
        pack_self,
        out_shape=[sds((4, 32, HEADS * HS), BF)] * 4,
        in_specs=[hbm] * 4,
        out_specs=[pl.BlockSpec(memory_space=pltpu.VMEM)] * 4,
        scratch_shapes=[pltpu.SemaphoreType.DMA((4, 4))],
    )(self_queries, self_keys, self_values, self_cotangent)
    task_shape = sds((TASKS, 4, BLK, HS), BF)
    vm = pl.BlockSpec(memory_space=pltpu.VMEM)
    sent = vmem_call(pack_text, task_shape)(
        text_queries, memory_keys, memory_values, text_cotangent
    )
    by_head = swap_heads(by_head)
    sent = vmem_call(
        pack_heads,
        task_shape,
        in_specs=[vm] * 4 + [hbm],
        out_specs=hbm,
        scratch_shapes=[pltpu.VMEM((HEADS, 4, BLK, HS), BF), pltpu.SemaphoreType.DMA],
        input_output_aliases={4: 0},
    )(*by_head, sent)
    held = lax.all_to_all(sent, "seq", split_axis=0, concat_axis=0, tiled=True)
    back = vmem_call(
        attend,
        sds((TASKS, 3 * BLK + 16, HS), BF),
        in_specs=[pl.BlockSpec(memory_space=pltpu.SMEM)] + [vm] * 5,
        scratch_shapes=[
            pltpu.VMEM((TASKS, HS, BLK), BF),
            pltpu.VMEM((patches, QB), F32),
            pltpu.VMEM((patches, QB), F32),
            pltpu.VMEM((patches, QB), BF),
            pltpu.VMEM((patches, HS), F32),
            pltpu.VMEM((patches, HS), F32),
            pltpu.VMEM((8, BLK), F32),
        ],
    )(window, key_row * sa, key_col * sb, key_id.astype(F32), q_info, held)

    back = lax.all_to_all(back, "seq", split_axis=0, concat_axis=0, tiled=True)
    part = sds((3, 32, HEADS * HS), BF)
    text_dq, mem_dk, mem_dv, slope_sum, *self_out = vmem_call(
        unpack_tasks,
        (
            sds(text_queries.shape, BF),
            sds(memory_keys.shape, BF),
            sds(memory_values.shape, BF),
            sds((2, 8, BLK), F32),
            *(part,) * 4,
        ),
    )(back)
    self_out = swap_heads(self_out)
    slope_sum, self_out[1] = lax.optimization_barrier((slope_sum, self_out[1]))
    slope_sum = jnp.sum(slope_sum[:, :HEADS], axis=2) / (slopes * (LOG2E * -patches))
    near, far, last = (
        lax.ppermute(slope_sum, "dp", [(i, i ^ gap) for i in range(4)])
        for gap in (1, 2, 3)
    )
    slope_grad = (slope_sum + near) + (far + last)
    shape = sds(self_queries.shape, BF)
    self_dq, self_dk, self_dv = vmem_call(unpack_self, (shape, shape, shape))(*self_out)
    return self_dq, self_dk, self_dv, slope_grad, text_dq, mem_dk, mem_dv


def solution(mesh):
    rows = P("dp", ("seq", "head"), None)
    cols = P("dp", "seq", "head")
    in_specs = (rows,) * 4 + (cols,) * 4 + (P(None, "head"),) + (P("dp", None),) * 3
    out_specs = (rows,) * 3 + (P(None, "head"),) + (cols,) * 3
    return jax.shard_map(local, mesh=mesh, in_specs=in_specs, out_specs=out_specs, check_vma=False)
```

```python
import functools
import jax
import jax.numpy as jnp
from jax import lax
from jax.experimental import pallas as pl
from jax.experimental.pallas import tpu as pltpu
from jax.sharding import PartitionSpec as P

MASK_FILL = -1e30
LOG2E = 1.4426950408889634
BF = jnp.bfloat16
F32 = jnp.float32

HEADS = 5
TEXT_TASKS = 10
TASKS = 16
BLK = 128
HS = 128
QB = 256
SIZES = (6, 9, 12, 16)


def vmem_call(body, out_shapes, **kw):
    return pl.pallas_call(
        body,
        out_shape=out_shapes,
        compiler_params=pltpu.CompilerParams(vmem_limit_bytes=24 * 2**20),
        **kw,
    )


def pack_self(q_ref, k_ref, v_ref, g_ref, *refs):
    outs, sems = refs[:4], refs[4]
    me = lax.axis_index("head")
    width = HEADS * HS
    copies = []
    for gap in (2, 1, 3, 0):
        at = pl.ds(pl.multiple_of((me ^ gap) * width, HS), width)
        for a, ref in enumerate((q_ref, k_ref, v_ref, g_ref)):
            copies.append(
                pltpu.make_async_copy(ref.at[0, :, at], outs[gap].at[a], sems.at[gap, a])
            )
            copies[-1].start()
    for copy in copies:
        copy.wait()


def pack_text(tq_ref, mk_ref, mv_ref, tg_ref, out_ref):
    for h in range(HEADS):
        cols = slice(h * HS, (h + 1) * HS)
        for j in range(2):
            t = 2 * h + j
            rows = slice(j * BLK, (j + 1) * BLK)
            out_ref[t, 0] = tq_ref[0, rows, cols]
            out_ref[t, 1] = mk_ref[0, :, cols]
            out_ref[t, 2] = mv_ref[0, :, cols]
            out_ref[t, 3] = tg_ref[0, rows, cols]
    out_ref[TEXT_TASKS:] = jnp.zeros((TASKS - TEXT_TASKS, 4, BLK, HS), BF)


def pack_heads(s0_ref, s1_ref, s2_ref, s3_ref, text_ref, out_ref, buf, sem):
    me = lax.axis_index("head")
    for h in range(HEADS):
        cols = slice(h * HS, (h + 1) * HS)
        for gap, ref in enumerate((s0_ref, s1_ref, s2_ref, s3_ref)):
            at = pl.ds(pl.multiple_of((me ^ gap) * 32, 32), 32)
            for a in range(4):
                buf[h, a, at] = ref[a, :, cols]
    copy = pltpu.make_async_copy(buf, out_ref.at[pl.ds(TEXT_TASKS, HEADS)], sem)
    copy.start()
    copy.wait()


def unpack_tasks(
    in_ref, tq_ref, mk_ref, mv_ref, slope_ref, s0_ref, s1_ref, s2_ref, s3_ref
):
    me = lax.axis_index("head")
    k, v = (slice(i * BLK, (i + 1) * BLK) for i in (1, 2))
    slope_ref[...] = jnp.zeros_like(slope_ref)
    for h in range(HEADS):
        cols = slice(h * HS, (h + 1) * HS)
        for j in range(2):
            tq_ref[0, j * BLK : (j + 1) * BLK, cols] = in_ref[2 * h + j, :BLK]
        mk = in_ref[2 * h, k].astype(F32) + in_ref[2 * h + 1, k].astype(F32)
        mv = in_ref[2 * h, v].astype(F32) + in_ref[2 * h + 1, v].astype(F32)
        mk_ref[0, :, cols] = mk.astype(BF)
        mv_ref[0, :, cols] = mv.astype(BF)
        for gap, ref in enumerate((s0_ref, s1_ref, s2_ref, s3_ref)):
            for a in range(3):
                at = pl.ds(pl.multiple_of(a * BLK + (me ^ gap) * 32, 32), 32)
                ref[a, :, cols] = in_ref[TEXT_TASKS + h, at]
        pieces = in_ref[TEXT_TASKS + h, 3 * BLK :].astype(F32)
        for i in range(2):
            whole = pieces[3 * i : 3 * i + 1] + pieces[3 * i + 1 : 3 * i + 2]
            slope_ref[i, h : h + 1] = whole + pieces[3 * i + 2 : 3 * i + 3]


def unpack_self(s0_ref, s1_ref, s2_ref, s3_ref, q_ref, k_ref, v_ref):
    me = lax.axis_index("head")
    width = HEADS * HS
    for gap, part in enumerate((s0_ref, s1_ref, s2_ref, s3_ref)):
        at = pl.ds(pl.multiple_of((me ^ gap) * width, HS), width)
        for a, ref in enumerate((q_ref, k_ref, v_ref)):
            ref[0, :, at] = part[a]


def attend(
    win_ref, page_ref, qi_ref, in_ref, out_ref,
    ka_ref, kb_ref, kp_ref, kt_buf, t_buf, d_buf, ds_buf, dk_acc, dv_acc, slope_ref,
):
    inv_root = HS ** (-0.5)
    blocks = TASKS * BLK // QB
    per = QB // BLK
    for s in range(TASKS):
        here = slice(s * BLK, (s + 1) * BLK)
        kt_buf[s] = in_ref[s, 1].T
        pos = (lax.broadcasted_iota(jnp.int32, (BLK, BLK), 0) + s * BLK).astype(F32)
        begin, width, inv, page = (jnp.full((BLK, BLK), v, F32) for v in (0.0, page_ref[3, 0], page_ref[4, 0], 0.0))
        for i in range(1, 4):
            later = pos >= page_ref[2, i]
            begin = jnp.where(later, page_ref[2, i], begin)
            width = jnp.where(later, page_ref[3, i], width)
            inv = jnp.where(later, page_ref[4, i], inv)
            page = jnp.where(later, float(i), page)
        off = pos - begin
        row = jnp.floor((off + 0.5) * inv)
        ka_ref[here] = row * page_ref[0, 0]
        kb_ref[here] = (off - row * width) * page_ref[1, 0]
        kp_ref[here] = page
    dk_acc[...] = jnp.zeros_like(dk_acc)
    dv_acc[...] = jnp.zeros_like(dv_acc)
    slope_ref[...] = jnp.zeros_like(slope_ref)
    nt = (((1,), (1,)), ((), ()))
    tn = (((0,), (0,)), ((), ()))

    def wide_lanes(tile):
        return jnp.concatenate([tile] * per, axis=1)

    def fold(x, op):
        return op(x.reshape(BLK // 8, 8, QB), axis=0)

    def work(b, first, tiles):
        start = first * BLK
        q = jnp.concatenate([in_ref[per * b + i, 0] for i in range(per)], axis=0)
        g = jnp.concatenate([in_ref[per * b + i, 3] for i in range(per)], axis=0)
        at = pl.ds(pl.multiple_of(b * QB, QB), QB)
        qa, qb, qp = (qi_ref[i : i + 1, at] for i in range(3))

        def rows(t):
            return pl.ds(pl.multiple_of(start + t * BLK, BLK), BLK)

        top = jnp.full((8, QB), -jnp.inf, F32)
        for t in range(tiles):
            r = rows(t)
            s = lax.dot_general(in_ref[first + t, 1], q, nt, preferred_element_type=F32)
            d_buf[t * BLK : (t + 1) * BLK] = lax.dot_general(
                in_ref[first + t, 2], g, nt, preferred_element_type=F32
            )
            gap = jnp.abs(wide_lanes(ka_ref[r]) - qa) + jnp.abs(wide_lanes(kb_ref[r]) - qb)
            logit = jnp.where(
                wide_lanes(kp_ref[r]) == qp, s * (inv_root * LOG2E) - gap, MASK_FILL
            )
            t_buf[t * BLK : (t + 1) * BLK] = logit
            top = jnp.maximum(top, fold(logit, jnp.max))
        top = jnp.max(top, axis=0, keepdims=True)
        total = jnp.zeros((8, QB), F32)
        dot = jnp.zeros((8, QB), F32)
        for t in range(tiles):
            here = slice(t * BLK, (t + 1) * BLK)
            e = jnp.exp2(t_buf[here] - top)
            total += fold(e, jnp.sum)
            dot += fold(e * d_buf[here], jnp.sum)
        total = jnp.sum(total, axis=0, keepdims=True)
        inv = 1.0 / total
        norm = top + jnp.log2(total)
        delta = jnp.sum(dot, axis=0, keepdims=True) * inv
        sa = jnp.zeros((8, QB), F32)
        sb = jnp.zeros((8, QB), F32)
        for t in range(tiles):
            here = slice(t * BLK, (t + 1) * BLK)
            r = rows(t)
            p = jnp.exp2(t_buf[here] - norm)
            ds = p * (d_buf[here] - delta)
            p_b = p.astype(BF)
            ds_b = ds.astype(BF)
            ds_buf[here] = ds_b
            sa += fold(ds * jnp.abs(wide_lanes(ka_ref[r]) - qa), jnp.sum)
            sb += fold(ds * jnp.abs(wide_lanes(kb_ref[r]) - qb), jnp.sum)
            dv_acc[r] += jnp.dot(p_b, g, preferred_element_type=F32)
            dk_acc[r] += jnp.dot(ds_b, q, preferred_element_type=F32)
        kt = jnp.concatenate([kt_buf[first + t] for t in range(tiles)], axis=1)
        dq = jnp.dot(kt, ds_buf[: tiles * BLK], preferred_element_type=F32).T
        dq = (dq * inv_root).astype(BF)
        for i in range(per):
            out_ref[per * b + i, :BLK] = dq[i * BLK : (i + 1) * BLK]
        for row, v in ((0, sa), (1, sb)):
            v = jnp.sum(v, axis=0, keepdims=True)
            slope_ref[row : row + 1] += sum(v[:, i * BLK : (i + 1) * BLK] for i in range(per))

    def step(b, _):
        for kind, tiles in enumerate(SIZES):

            @pl.when(win_ref[1, b] == kind)
            def _(tiles=tiles):
                work(b, win_ref[0, b], tiles)

        return 0

    lax.fori_loop(0, blocks, step, 0)
    line = lax.broadcasted_iota(jnp.int32, (16, BLK), 0)
    pieces = jnp.zeros((16, BLK), F32)
    for row in range(2):
        rest = jnp.broadcast_to(slope_ref[row : row + 1], (16, BLK))
        for i in range(3):
            piece = rest.astype(BF).astype(F32)
            rest = rest - piece
            pieces = jnp.where(line == 3 * row + i, piece, pieces)
    pieces = pieces.astype(BF)
    for s in range(TASKS):
        here = slice(s * BLK, (s + 1) * BLK)
        out_ref[s, BLK : 2 * BLK] = (dk_acc[here] * inv_root).astype(BF)
        out_ref[s, 2 * BLK : 3 * BLK] = dv_acc[here].astype(BF)
        out_ref[s, 3 * BLK :] = pieces


def local(
    self_queries, self_keys, self_values, self_cotangent,
    text_queries, memory_keys, memory_values, text_cotangent,
    slopes, page_counts, page_cols, text_page,
):
    patches = TASKS * BLK
    sds = jax.ShapeDtypeStruct
    task = lax.axis_index("seq")
    is_text = task < TEXT_TASKS

    counts, widths = page_counts[0], page_cols[0]
    ends = [counts[0]]
    for i in range(1, 4):
        ends.append(ends[-1] + counts[i])
    starts = [jnp.int32(0)] + ends[:-1]

    def by_page(ids, per_page):
        out = jnp.broadcast_to(per_page[3], ids.shape)
        for i in (2, 1, 0):
            out = jnp.where(ids == i, per_page[i], out)
        return out

    def layout(pos):
        ids = sum((pos >= e).astype(jnp.int32) for e in ends[:3])
        width = by_page(ids, [widths[i] for i in range(4)])
        off = (pos - by_page(ids, starts)).astype(F32)
        row = jnp.floor((off + 0.5) / width.astype(F32))
        return ids, row, off - row * width.astype(F32)

    own = jnp.clip(task - TEXT_TASKS, 0, HEADS - 1)
    slope = jnp.where(is_text, 0.0, lax.dynamic_slice_in_dim(slopes, own, 1, 1)[:, 0])
    sa, sb = slope[0] * LOG2E, slope[1] * LOG2E
    as_row = lambda values: jnp.stack([jnp.asarray(v, F32) for v in values])
    pages = jnp.stack(
        [
            as_row([sa] * 4),
            as_row([sb] * 4),
            as_row(starts),
            widths.astype(F32),
            1.0 / widths.astype(F32),
        ]
    )
    pos_id, pos_row, pos_col = layout(jnp.arange(patches, dtype=jnp.int32))
    halves = text_page[0].reshape(TASKS, 2, BLK)
    text_id = lax.dynamic_index_in_dim(halves, task % 2, 1, keepdims=False).reshape(-1)
    q_id = jnp.where(is_text, text_id, pos_id)
    q_info = jnp.stack([pos_row * sa, pos_col * sb, q_id.astype(F32)])
    q_info = jnp.concatenate([q_info, jnp.zeros((5, patches), F32)])
    blocks = q_id.reshape(-1, QB)
    low = by_page(blocks[:, 0], starts) // BLK
    high = (by_page(blocks[:, -1], ends) + BLK - 1) // BLK
    first, kind = jnp.zeros_like(low), jnp.full_like(low, len(SIZES) - 1)
    for i in reversed(range(len(SIZES) - 1)):
        at = jnp.minimum(low, TASKS - SIZES[i])
        fits = high <= at + SIZES[i]
        first, kind = jnp.where(fits, at, first), jnp.where(fits, i, kind)
    window = jnp.stack([first, kind])

    def swap_heads(parts):
        own, out = parts[0], [None] * 4
        for gap in (2, 1, 3):
            swap = [(i, i ^ gap) for i in range(4)]
            out[gap] = lax.ppermute(parts[gap], "head", swap)
        return [own] + out[1:]

    hbm = pl.BlockSpec(memory_space=pltpu.HBM)
    by_head = pl.pallas_call(
        pack_self,
        out_shape=[sds((4, 32, HEADS * HS), BF)] * 4,
        in_specs=[hbm] * 4,
        out_specs=[pl.BlockSpec(memory_space=pltpu.VMEM)] * 4,
        scratch_shapes=[pltpu.SemaphoreType.DMA((4, 4))],
    )(self_queries, self_keys, self_values, self_cotangent)
    task_shape = sds((TASKS, 4, BLK, HS), BF)
    vm = pl.BlockSpec(memory_space=pltpu.VMEM)
    sent = vmem_call(pack_text, task_shape)(
        text_queries, memory_keys, memory_values, text_cotangent
    )
    by_head = swap_heads(by_head)
    sent = vmem_call(
        pack_heads,
        task_shape,
        in_specs=[vm] * 4 + [hbm],
        out_specs=hbm,
        scratch_shapes=[pltpu.VMEM((HEADS, 4, BLK, HS), BF), pltpu.SemaphoreType.DMA],
        input_output_aliases={4: 0},
    )(*by_head, sent)
    held = lax.all_to_all(sent, "seq", split_axis=0, concat_axis=0, tiled=True)
    back = vmem_call(
        attend,
        sds((TASKS, 3 * BLK + 16, HS), BF),
        in_specs=[pl.BlockSpec(memory_space=pltpu.SMEM)] * 2 + [vm] * 2,
        scratch_shapes=[
            pltpu.VMEM((patches, BLK), F32),
            pltpu.VMEM((patches, BLK), F32),
            pltpu.VMEM((patches, BLK), F32),
            pltpu.VMEM((TASKS, HS, BLK), BF),
            pltpu.VMEM((patches, QB), F32),
            pltpu.VMEM((patches, QB), F32),
            pltpu.VMEM((patches, QB), BF),
            pltpu.VMEM((patches, HS), F32),
            pltpu.VMEM((patches, HS), F32),
            pltpu.VMEM((8, BLK), F32),
        ],
    )(window, pages, q_info, held)

    back = lax.all_to_all(back, "seq", split_axis=0, concat_axis=0, tiled=True)
    part = sds((3, 32, HEADS * HS), BF)
    text_dq, mem_dk, mem_dv, slope_sum, *self_out = vmem_call(
        unpack_tasks,
        (
            sds(text_queries.shape, BF),
            sds(memory_keys.shape, BF),
            sds(memory_values.shape, BF),
            sds((2, 8, BLK), F32),
            *(part,) * 4,
        ),
    )(back)
    slope_sum = slope_sum + lax.ppermute(slope_sum, "dp", [(i, i ^ 1) for i in range(4)])
    self_out = swap_heads(self_out)
    slope_sum, self_out[1] = lax.optimization_barrier((slope_sum, self_out[1]))
    slope_sum = slope_sum + lax.ppermute(slope_sum, "dp", [(i, i ^ 2) for i in range(4)])
    slope_sum = jnp.sum(slope_sum[:, :HEADS], axis=2)
    slope_grad = slope_sum / (slopes * (LOG2E * -patches))
    shape = sds(self_queries.shape, BF)
    self_dq, self_dk, self_dv = vmem_call(unpack_self, (shape, shape, shape))(*self_out)
    return self_dq, self_dk, self_dv, slope_grad, text_dq, mem_dk, mem_dv


def solution(mesh):
    rows = P("dp", ("seq", "head"), None)
    cols = P("dp", "seq", "head")
    in_specs = (rows,) * 4 + (cols,) * 4 + (P(None, "head"),) + (P("dp", None),) * 3
    out_specs = (rows,) * 3 + (P(None, "head"),) + (cols,) * 3
    return jax.shard_map(local, mesh=mesh, in_specs=in_specs, out_specs=out_specs, check_vma=False)
```

```python
import functools
import jax
import jax.numpy as jnp
from jax import lax
from jax.experimental import pallas as pl
from jax.experimental.pallas import tpu as pltpu
from jax.sharding import PartitionSpec as P

MASK_FILL = -1e30
LOG2E = 1.4426950408889634
BF = jnp.bfloat16
F32 = jnp.float32

HEADS = 5
TEXT_TASKS = 10
TASKS = 16
BLK = 128
HS = 128
QB = 256
SIZES = (6, 9, 12, 16)


def vmem_call(body, out_shapes, **kw):
    return pl.pallas_call(
        body,
        out_shape=out_shapes,
        compiler_params=pltpu.CompilerParams(vmem_limit_bytes=24 * 2**20),
        **kw,
    )


def pack_self(q_ref, k_ref, v_ref, g_ref, *refs):
    outs, sems = refs[:4], refs[4]
    me = lax.axis_index("head")
    width = HEADS * HS
    copies = []
    for gap in (2, 1, 3, 0):
        at = pl.ds(pl.multiple_of((me ^ gap) * width, HS), width)
        for a, ref in enumerate((q_ref, k_ref, v_ref, g_ref)):
            copies.append(
                pltpu.make_async_copy(ref.at[0, :, at], outs[gap].at[a], sems.at[gap, a])
            )
            copies[-1].start()
    for copy in copies:
        copy.wait()


def pack_text(tq_ref, mk_ref, mv_ref, tg_ref, out_ref):
    for h in range(HEADS):
        cols = slice(h * HS, (h + 1) * HS)
        for j in range(2):
            t = 2 * h + j
            rows = slice(j * BLK, (j + 1) * BLK)
            out_ref[t, 0] = tq_ref[0, rows, cols]
            out_ref[t, 1] = mk_ref[0, :, cols]
            out_ref[t, 2] = mv_ref[0, :, cols]
            out_ref[t, 3] = tg_ref[0, rows, cols]
    out_ref[TEXT_TASKS:] = jnp.zeros((TASKS - TEXT_TASKS, 4, BLK, HS), BF)


def pack_heads(s0_ref, s1_ref, s2_ref, s3_ref, text_ref, out_ref, buf, sem):
    me = lax.axis_index("head")
    for h in range(HEADS):
        cols = slice(h * HS, (h + 1) * HS)
        for gap, ref in enumerate((s0_ref, s1_ref, s2_ref, s3_ref)):
            at = pl.ds(pl.multiple_of((me ^ gap) * 32, 32), 32)
            for a in range(4):
                buf[h, a, at] = ref[a, :, cols]
    copy = pltpu.make_async_copy(buf, out_ref.at[pl.ds(TEXT_TASKS, HEADS)], sem)
    copy.start()
    copy.wait()


def unpack_tasks(in_ref, tq_ref, mk_ref, mv_ref, slope_ref, self_ref):
    k, v = (slice(i * BLK, (i + 1) * BLK) for i in (1, 2))
    slope_ref[...] = jnp.zeros_like(slope_ref)
    for h in range(HEADS):
        cols = slice(h * HS, (h + 1) * HS)
        for a in range(3):
            for x in range(4):
                at = a * BLK + x * 32
                self_ref[x, a, :, cols] = in_ref[TEXT_TASKS + h, at : at + 32]
        for j in range(2):
            tq_ref[0, j * BLK : (j + 1) * BLK, cols] = in_ref[2 * h + j, :BLK]
        mk = in_ref[2 * h, k].astype(F32) + in_ref[2 * h + 1, k].astype(F32)
        mv = in_ref[2 * h, v].astype(F32) + in_ref[2 * h + 1, v].astype(F32)
        mk_ref[0, :, cols] = mk.astype(BF)
        mv_ref[0, :, cols] = mv.astype(BF)
        pieces = in_ref[TEXT_TASKS + h, 3 * BLK :].astype(F32)
        for i in range(2):
            whole = pieces[3 * i : 3 * i + 1] + pieces[3 * i + 1 : 3 * i + 2]
            slope_ref[i, h : h + 1] = whole + pieces[3 * i + 2 : 3 * i + 3]


def unpack_self(in_ref, q_ref, k_ref, v_ref):
    width = HEADS * HS
    for x in range(4):
        for a, ref in enumerate((q_ref, k_ref, v_ref)):
            ref[0, :, x * width : (x + 1) * width] = in_ref[x, a]


def attend(
    win_ref, page_ref, qi_ref, in_ref, out_ref,
    ka_ref, kb_ref, kp_ref, kt_buf, t_buf, d_buf, ds_buf, dk_acc, dv_acc, slope_ref,
):
    inv_root = HS ** (-0.5)
    blocks = TASKS * BLK // QB
    per = QB // BLK
    for s in range(TASKS):
        here = slice(s * BLK, (s + 1) * BLK)
        kt_buf[s] = in_ref[s, 1].T
        pos = (lax.broadcasted_iota(jnp.int32, (BLK, BLK), 0) + s * BLK).astype(F32)
        begin, width, inv, page = (jnp.full((BLK, BLK), v, F32) for v in (0.0, page_ref[3, 0], page_ref[4, 0], 0.0))
        for i in range(1, 4):
            later = pos >= page_ref[2, i]
            begin = jnp.where(later, page_ref[2, i], begin)
            width = jnp.where(later, page_ref[3, i], width)
            inv = jnp.where(later, page_ref[4, i], inv)
            page = jnp.where(later, float(i), page)
        off = pos - begin
        row = jnp.floor((off + 0.5) * inv)
        ka_ref[here] = row * page_ref[0, 0]
        kb_ref[here] = (off - row * width) * page_ref[1, 0]
        kp_ref[here] = page
    dk_acc[...] = jnp.zeros_like(dk_acc)
    dv_acc[...] = jnp.zeros_like(dv_acc)
    slope_ref[...] = jnp.zeros_like(slope_ref)
    nt = (((1,), (1,)), ((), ()))
    tn = (((0,), (0,)), ((), ()))

    def wide_lanes(tile):
        return jnp.concatenate([tile] * per, axis=1)

    def fold(x, op):
        return op(x.reshape(BLK // 8, 8, QB), axis=0)

    def work(b, first, tiles):
        start = first * BLK
        q = jnp.concatenate([in_ref[per * b + i, 0] for i in range(per)], axis=0)
        g = jnp.concatenate([in_ref[per * b + i, 3] for i in range(per)], axis=0)
        at = pl.ds(pl.multiple_of(b * QB, QB), QB)
        qa, qb, qp = (qi_ref[i : i + 1, at] for i in range(3))

        def rows(t):
            return pl.ds(pl.multiple_of(start + t * BLK, BLK), BLK)

        top = jnp.full((8, QB), -jnp.inf, F32)
        for t in range(tiles):
            r = rows(t)
            s = lax.dot_general(in_ref[first + t, 1], q, nt, preferred_element_type=F32)
            d_buf[t * BLK : (t + 1) * BLK] = lax.dot_general(
                in_ref[first + t, 2], g, nt, preferred_element_type=F32
            )
            gap = jnp.abs(wide_lanes(ka_ref[r]) - qa) + jnp.abs(wide_lanes(kb_ref[r]) - qb)
            logit = jnp.where(
                wide_lanes(kp_ref[r]) == qp, s * (inv_root * LOG2E) - gap, MASK_FILL
            )
            t_buf[t * BLK : (t + 1) * BLK] = logit
            top = jnp.maximum(top, fold(logit, jnp.max))
        top = jnp.max(top, axis=0, keepdims=True)
        total = jnp.zeros((8, QB), F32)
        dot = jnp.zeros((8, QB), F32)
        for t in range(tiles):
            here = slice(t * BLK, (t + 1) * BLK)
            e = jnp.exp2(t_buf[here] - top)
            total += fold(e, jnp.sum)
            dot += fold(e * d_buf[here], jnp.sum)
        total = jnp.sum(total, axis=0, keepdims=True)
        inv = 1.0 / total
        norm = top + jnp.log2(total)
        delta = jnp.sum(dot, axis=0, keepdims=True) * inv
        sa = jnp.zeros((8, QB), F32)
        sb = jnp.zeros((8, QB), F32)
        for t in range(tiles):
            here = slice(t * BLK, (t + 1) * BLK)
            r = rows(t)
            p = jnp.exp2(t_buf[here] - norm)
            ds = p * (d_buf[here] - delta)
            p_b = p.astype(BF)
            ds_b = ds.astype(BF)
            ds_buf[here] = ds_b
            sa += fold(ds * jnp.abs(wide_lanes(ka_ref[r]) - qa), jnp.sum)
            sb += fold(ds * jnp.abs(wide_lanes(kb_ref[r]) - qb), jnp.sum)
            dv_acc[r] += jnp.dot(p_b, g, preferred_element_type=F32)
            dk_acc[r] += jnp.dot(ds_b, q, preferred_element_type=F32)
        kt = jnp.concatenate([kt_buf[first + t] for t in range(tiles)], axis=1)
        dq = jnp.dot(kt, ds_buf[: tiles * BLK], preferred_element_type=F32).T
        dq = (dq * inv_root).astype(BF)
        for i in range(per):
            out_ref[per * b + i, :BLK] = dq[i * BLK : (i + 1) * BLK]
        for row, v in ((0, sa), (1, sb)):
            v = jnp.sum(v, axis=0, keepdims=True)
            slope_ref[row : row + 1] += sum(v[:, i * BLK : (i + 1) * BLK] for i in range(per))

    def step(b, _):
        for kind, tiles in enumerate(SIZES):

            @pl.when(win_ref[1, b] == kind)
            def _(tiles=tiles):
                work(b, win_ref[0, b], tiles)

        return 0

    lax.fori_loop(0, blocks, step, 0)
    line = lax.broadcasted_iota(jnp.int32, (16, BLK), 0)
    pieces = jnp.zeros((16, BLK), F32)
    for row in range(2):
        rest = jnp.broadcast_to(slope_ref[row : row + 1], (16, BLK))
        for i in range(3):
            piece = rest.astype(BF).astype(F32)
            rest = rest - piece
            pieces = jnp.where(line == 3 * row + i, piece, pieces)
    pieces = pieces.astype(BF)
    for s in range(TASKS):
        here = slice(s * BLK, (s + 1) * BLK)
        out_ref[s, BLK : 2 * BLK] = (dk_acc[here] * inv_root).astype(BF)
        out_ref[s, 2 * BLK : 3 * BLK] = dv_acc[here].astype(BF)
        out_ref[s, 3 * BLK :] = pieces


def local(
    self_queries, self_keys, self_values, self_cotangent,
    text_queries, memory_keys, memory_values, text_cotangent,
    slopes, page_counts, page_cols, text_page,
):
    patches = TASKS * BLK
    sds = jax.ShapeDtypeStruct
    task = lax.axis_index("seq")
    is_text = task < TEXT_TASKS

    counts, widths = page_counts[0], page_cols[0]
    ends = [counts[0]]
    for i in range(1, 4):
        ends.append(ends[-1] + counts[i])
    starts = [jnp.int32(0)] + ends[:-1]

    def by_page(ids, per_page):
        out = jnp.broadcast_to(per_page[3], ids.shape)
        for i in (2, 1, 0):
            out = jnp.where(ids == i, per_page[i], out)
        return out

    def layout(pos):
        ids = sum((pos >= e).astype(jnp.int32) for e in ends[:3])
        width = by_page(ids, [widths[i] for i in range(4)])
        off = (pos - by_page(ids, starts)).astype(F32)
        row = jnp.floor((off + 0.5) / width.astype(F32))
        return ids, row, off - row * width.astype(F32)

    own = jnp.clip(task - TEXT_TASKS, 0, HEADS - 1)
    slope = jnp.where(is_text, 0.0, lax.dynamic_slice_in_dim(slopes, own, 1, 1)[:, 0])
    sa, sb = slope[0] * LOG2E, slope[1] * LOG2E
    as_row = lambda values: jnp.stack([jnp.asarray(v, F32) for v in values])
    pages = jnp.stack(
        [
            as_row([sa] * 4),
            as_row([sb] * 4),
            as_row(starts),
            widths.astype(F32),
            1.0 / widths.astype(F32),
        ]
    )
    pos_id, pos_row, pos_col = layout(jnp.arange(patches, dtype=jnp.int32))
    halves = text_page[0].reshape(TASKS, 2, BLK)
    text_id = lax.dynamic_index_in_dim(halves, task % 2, 1, keepdims=False).reshape(-1)
    q_id = jnp.where(is_text, text_id, pos_id)
    q_info = jnp.stack([pos_row * sa, pos_col * sb, q_id.astype(F32)])
    q_info = jnp.concatenate([q_info, jnp.zeros((5, patches), F32)])
    blocks = q_id.reshape(-1, QB)
    low = by_page(blocks[:, 0], starts) // BLK
    high = (by_page(blocks[:, -1], ends) + BLK - 1) // BLK
    first, kind = jnp.zeros_like(low), jnp.full_like(low, len(SIZES) - 1)
    for i in reversed(range(len(SIZES) - 1)):
        at = jnp.minimum(low, TASKS - SIZES[i])
        fits = high <= at + SIZES[i]
        first, kind = jnp.where(fits, at, first), jnp.where(fits, i, kind)
    window = jnp.stack([first, kind])

    def swap_heads(parts):
        own, out = parts[0], [None] * 4
        for gap in (2, 1, 3):
            swap = [(i, i ^ gap) for i in range(4)]
            out[gap] = lax.ppermute(parts[gap], "head", swap)
        return [own] + out[1:]

    hbm = pl.BlockSpec(memory_space=pltpu.HBM)
    by_head = pl.pallas_call(
        pack_self,
        out_shape=[sds((4, 32, HEADS * HS), BF)] * 4,
        in_specs=[hbm] * 4,
        out_specs=[pl.BlockSpec(memory_space=pltpu.VMEM)] * 4,
        scratch_shapes=[pltpu.SemaphoreType.DMA((4, 4))],
    )(self_queries, self_keys, self_values, self_cotangent)
    task_shape = sds((TASKS, 4, BLK, HS), BF)
    vm = pl.BlockSpec(memory_space=pltpu.VMEM)
    sent = vmem_call(pack_text, task_shape)(
        text_queries, memory_keys, memory_values, text_cotangent
    )
    by_head = swap_heads(by_head)
    sent = vmem_call(
        pack_heads,
        task_shape,
        in_specs=[vm] * 4 + [hbm],
        out_specs=hbm,
        scratch_shapes=[pltpu.VMEM((HEADS, 4, BLK, HS), BF), pltpu.SemaphoreType.DMA],
        input_output_aliases={4: 0},
    )(*by_head, sent)
    held = lax.all_to_all(sent, "seq", split_axis=0, concat_axis=0, tiled=True)
    back = vmem_call(
        attend,
        sds((TASKS, 3 * BLK + 16, HS), BF),
        in_specs=[pl.BlockSpec(memory_space=pltpu.SMEM)] * 2 + [vm] * 2,
        scratch_shapes=[
            pltpu.VMEM((patches, BLK), F32),
            pltpu.VMEM((patches, BLK), F32),
            pltpu.VMEM((patches, BLK), F32),
            pltpu.VMEM((TASKS, HS, BLK), BF),
            pltpu.VMEM((patches, QB), F32),
            pltpu.VMEM((patches, QB), F32),
            pltpu.VMEM((patches, QB), BF),
            pltpu.VMEM((patches, HS), F32),
            pltpu.VMEM((patches, HS), F32),
            pltpu.VMEM((8, BLK), F32),
        ],
    )(window, pages, q_info, held)

    back = lax.all_to_all(back, "seq", split_axis=0, concat_axis=0, tiled=True)
    text_dq, mem_dk, mem_dv, slope_sum, self_out = vmem_call(
        unpack_tasks,
        (
            sds(text_queries.shape, BF),
            sds(memory_keys.shape, BF),
            sds(memory_values.shape, BF),
            sds((2, 8, BLK), F32),
            sds((4, 3, 32, HEADS * HS), BF),
        ),
    )(back)
    self_out = lax.all_to_all(self_out, "head", split_axis=0, concat_axis=0, tiled=True)
    for gap in (1, 2):
        swap = [(i, i ^ gap) for i in range(4)]
        slope_sum = slope_sum + lax.ppermute(slope_sum, "dp", swap)
    slope_sum = jnp.sum(slope_sum[:, :HEADS], axis=2)
    slope_grad = slope_sum / (slopes * (LOG2E * -patches))
    shape = sds(self_queries.shape, BF)
    self_dq, self_dk, self_dv = vmem_call(unpack_self, (shape, shape, shape))(self_out)
    return self_dq, self_dk, self_dv, slope_grad, text_dq, mem_dk, mem_dv


def solution(mesh):
    rows = P("dp", ("seq", "head"), None)
    cols = P("dp", "seq", "head")
    in_specs = (rows,) * 4 + (cols,) * 4 + (P(None, "head"),) + (P("dp", None),) * 3
    out_specs = (rows,) * 3 + (P(None, "head"),) + (cols,) * 3
    return jax.shard_map(local, mesh=mesh, in_specs=in_specs, out_specs=out_specs, check_vma=False)
```

```python
import functools
import jax
import jax.numpy as jnp
from jax import lax
from jax.experimental import pallas as pl
from jax.experimental.pallas import tpu as pltpu
from jax.sharding import PartitionSpec as P

MASK_FILL = -1e30
LOG2E = 1.4426950408889634
BF = jnp.bfloat16
F32 = jnp.float32

HEADS = 5
TEXT_TASKS = 10
TASKS = 16
BLK = 128
HS = 128
QB = 256
SIZES = (6, 9, 12, 16)


def vmem_call(body, out_shapes, **kw):
    return pl.pallas_call(
        body,
        out_shape=out_shapes,
        compiler_params=pltpu.CompilerParams(vmem_limit_bytes=24 * 2**20),
        **kw,
    )


def pack_self(q_ref, k_ref, v_ref, g_ref, *refs):
    outs, sems = refs[:4], refs[4]
    me = lax.axis_index("head")
    width = HEADS * HS
    copies = []
    for gap in (2, 1, 3, 0):
        at = pl.ds(pl.multiple_of((me ^ gap) * width, HS), width)
        for a, ref in enumerate((q_ref, k_ref, v_ref, g_ref)):
            copies.append(
                pltpu.make_async_copy(ref.at[0, :, at], outs[gap].at[a], sems.at[gap, a])
            )
            copies[-1].start()
    for copy in copies:
        copy.wait()


def pack_text(tq_ref, mk_ref, mv_ref, tg_ref, out_ref):
    for h in range(HEADS):
        cols = slice(h * HS, (h + 1) * HS)
        for j in range(2):
            t = 2 * h + j
            rows = slice(j * BLK, (j + 1) * BLK)
            out_ref[t, 0] = tq_ref[0, rows, cols]
            out_ref[t, 1] = mk_ref[0, :, cols]
            out_ref[t, 2] = mv_ref[0, :, cols]
            out_ref[t, 3] = tg_ref[0, rows, cols]
    out_ref[TEXT_TASKS:] = jnp.zeros((TASKS - TEXT_TASKS, 4, BLK, HS), BF)


def pack_heads(s0_ref, s1_ref, s2_ref, s3_ref, text_ref, out_ref, buf, sem):
    me = lax.axis_index("head")
    for h in range(HEADS):
        cols = slice(h * HS, (h + 1) * HS)
        for gap, ref in enumerate((s0_ref, s1_ref, s2_ref, s3_ref)):
            at = pl.ds(pl.multiple_of((me ^ gap) * 32, 32), 32)
            for a in range(4):
                buf[h, a, at] = ref[a, :, cols]
    copy = pltpu.make_async_copy(buf, out_ref.at[pl.ds(TEXT_TASKS, HEADS)], sem)
    copy.start()
    copy.wait()


def unpack_tasks(in_ref, tq_ref, mk_ref, mv_ref, self_ref):
    k, v = (slice(i * BLK, (i + 1) * BLK) for i in (1, 2))
    for h in range(HEADS):
        cols = slice(h * HS, (h + 1) * HS)
        for a in range(3):
            for x in range(4):
                at = a * BLK + x * 32
                self_ref[x, a, :, cols] = in_ref[TEXT_TASKS + h, at : at + 32]
        for j in range(2):
            tq_ref[0, j * BLK : (j + 1) * BLK, cols] = in_ref[2 * h + j, :BLK]
        mk = in_ref[2 * h, k].astype(F32) + in_ref[2 * h + 1, k].astype(F32)
        mv = in_ref[2 * h, v].astype(F32) + in_ref[2 * h + 1, v].astype(F32)
        mk_ref[0, :, cols] = mk.astype(BF)
        mv_ref[0, :, cols] = mv.astype(BF)


def unpack_self(in_ref, q_ref, k_ref, v_ref):
    width = HEADS * HS
    for x in range(4):
        for a, ref in enumerate((q_ref, k_ref, v_ref)):
            ref[0, :, x * width : (x + 1) * width] = in_ref[x, a]


def attend(
    win_ref, page_ref, qi_ref, in_ref, out_ref, sum_ref,
    ka_ref, kb_ref, kp_ref, kt_buf, t_buf, d_buf, ds_buf, dk_acc, dv_acc, slope_ref,
):
    inv_root = HS ** (-0.5)
    blocks = TASKS * BLK // QB
    per = QB // BLK
    for s in range(TASKS):
        here = slice(s * BLK, (s + 1) * BLK)
        kt_buf[s] = in_ref[s, 1].T
        pos = (lax.broadcasted_iota(jnp.int32, (BLK, BLK), 0) + s * BLK).astype(F32)
        begin, width, inv, page = (jnp.full((BLK, BLK), v, F32) for v in (0.0, page_ref[3, 0], page_ref[4, 0], 0.0))
        for i in range(1, 4):
            later = pos >= page_ref[2, i]
            begin = jnp.where(later, page_ref[2, i], begin)
            width = jnp.where(later, page_ref[3, i], width)
            inv = jnp.where(later, page_ref[4, i], inv)
            page = jnp.where(later, float(i), page)
        off = pos - begin
        row = jnp.floor((off + 0.5) * inv)
        ka_ref[here] = row * page_ref[0, 0]
        kb_ref[here] = (off - row * width) * page_ref[1, 0]
        kp_ref[here] = page
    dk_acc[...] = jnp.zeros_like(dk_acc)
    dv_acc[...] = jnp.zeros_like(dv_acc)
    slope_ref[...] = jnp.zeros_like(slope_ref)
    nt = (((1,), (1,)), ((), ()))
    tn = (((0,), (0,)), ((), ()))

    def wide_lanes(tile):
        return jnp.concatenate([tile] * per, axis=1)

    def fold(x, op):
        return op(x.reshape(BLK // 8, 8, QB), axis=0)

    def work(b, first, tiles):
        start = first * BLK
        q = jnp.concatenate([in_ref[per * b + i, 0] for i in range(per)], axis=0)
        g = jnp.concatenate([in_ref[per * b + i, 3] for i in range(per)], axis=0)
        at = pl.ds(pl.multiple_of(b * QB, QB), QB)
        qa, qb, qp = (qi_ref[i : i + 1, at] for i in range(3))

        def rows(t):
            return pl.ds(pl.multiple_of(start + t * BLK, BLK), BLK)

        top = jnp.full((8, QB), -jnp.inf, F32)
        for t in range(tiles):
            r = rows(t)
            s = lax.dot_general(in_ref[first + t, 1], q, nt, preferred_element_type=F32)
            d_buf[t * BLK : (t + 1) * BLK] = lax.dot_general(
                in_ref[first + t, 2], g, nt, preferred_element_type=F32
            )
            gap = jnp.abs(wide_lanes(ka_ref[r]) - qa) + jnp.abs(wide_lanes(kb_ref[r]) - qb)
            logit = jnp.where(
                wide_lanes(kp_ref[r]) == qp, s * (inv_root * LOG2E) - gap, MASK_FILL
            )
            t_buf[t * BLK : (t + 1) * BLK] = logit
            top = jnp.maximum(top, fold(logit, jnp.max))
        top = jnp.max(top, axis=0, keepdims=True)
        total = jnp.zeros((8, QB), F32)
        dot = jnp.zeros((8, QB), F32)
        for t in range(tiles):
            here = slice(t * BLK, (t + 1) * BLK)
            e = jnp.exp2(t_buf[here] - top)
            total += fold(e, jnp.sum)
            dot += fold(e * d_buf[here], jnp.sum)
        total = jnp.sum(total, axis=0, keepdims=True)
        inv = 1.0 / total
        norm = top + jnp.log2(total)
        delta = jnp.sum(dot, axis=0, keepdims=True) * inv
        sa = jnp.zeros((8, QB), F32)
        sb = jnp.zeros((8, QB), F32)
        for t in range(tiles):
            here = slice(t * BLK, (t + 1) * BLK)
            r = rows(t)
            p = jnp.exp2(t_buf[here] - norm)
            ds = p * (d_buf[here] - delta)
            p_b = p.astype(BF)
            ds_b = ds.astype(BF)
            ds_buf[here] = ds_b
            sa += fold(ds * jnp.abs(wide_lanes(ka_ref[r]) - qa), jnp.sum)
            sb += fold(ds * jnp.abs(wide_lanes(kb_ref[r]) - qb), jnp.sum)
            dv_acc[r] += jnp.dot(p_b, g, preferred_element_type=F32)
            dk_acc[r] += jnp.dot(ds_b, q, preferred_element_type=F32)
        kt = jnp.concatenate([kt_buf[first + t] for t in range(tiles)], axis=1)
        dq = jnp.dot(kt, ds_buf[: tiles * BLK], preferred_element_type=F32).T
        dq = (dq * inv_root).astype(BF)
        for i in range(per):
            out_ref[per * b + i, :BLK] = dq[i * BLK : (i + 1) * BLK]
        for row, v in ((0, sa), (1, sb)):
            v = jnp.sum(v, axis=0, keepdims=True)
            slope_ref[row : row + 1] += sum(v[:, i * BLK : (i + 1) * BLK] for i in range(per))

    def step(b, _):
        for kind, tiles in enumerate(SIZES):

            @pl.when(win_ref[1, b] == kind)
            def _(tiles=tiles):
                work(b, win_ref[0, b], tiles)

        return 0

    lax.fori_loop(0, blocks, step, 0)
    line = lax.broadcasted_iota(jnp.int32, (BLK, BLK), 0)
    slot = win_ref[2, 0]
    sum_ref[...] = jnp.where(
        line == slot, slope_ref[0:1], jnp.where(line == slot + 1, slope_ref[1:2], 0.0)
    )
    for s in range(TASKS):
        here = slice(s * BLK, (s + 1) * BLK)
        out_ref[s, BLK : 2 * BLK] = (dk_acc[here] * inv_root).astype(BF)
        out_ref[s, 2 * BLK : 3 * BLK] = dv_acc[here].astype(BF)


def local(
    self_queries, self_keys, self_values, self_cotangent,
    text_queries, memory_keys, memory_values, text_cotangent,
    slopes, page_counts, page_cols, text_page,
):
    patches = TASKS * BLK
    sds = jax.ShapeDtypeStruct
    task = lax.axis_index("seq")
    is_text = task < TEXT_TASKS

    counts, widths = page_counts[0], page_cols[0]
    ends = [counts[0]]
    for i in range(1, 4):
        ends.append(ends[-1] + counts[i])
    starts = [jnp.int32(0)] + ends[:-1]

    def by_page(ids, per_page):
        out = jnp.broadcast_to(per_page[3], ids.shape)
        for i in (2, 1, 0):
            out = jnp.where(ids == i, per_page[i], out)
        return out

    def layout(pos):
        ids = sum((pos >= e).astype(jnp.int32) for e in ends[:3])
        width = by_page(ids, [widths[i] for i in range(4)])
        off = (pos - by_page(ids, starts)).astype(F32)
        row = jnp.floor((off + 0.5) / width.astype(F32))
        return ids, row, off - row * width.astype(F32)

    own = jnp.clip(task - TEXT_TASKS, 0, HEADS - 1)
    slope = jnp.where(is_text, 0.0, lax.dynamic_slice_in_dim(slopes, own, 1, 1)[:, 0])
    sa, sb = slope[0] * LOG2E, slope[1] * LOG2E
    as_row = lambda values: jnp.stack([jnp.asarray(v, F32) for v in values])
    pages = jnp.stack(
        [
            as_row([sa] * 4),
            as_row([sb] * 4),
            as_row(starts),
            widths.astype(F32),
            1.0 / widths.astype(F32),
        ]
    )
    pos_id, pos_row, pos_col = layout(jnp.arange(patches, dtype=jnp.int32))
    halves = text_page[0].reshape(TASKS, 2, BLK)
    text_id = lax.dynamic_index_in_dim(halves, task % 2, 1, keepdims=False).reshape(-1)
    q_id = jnp.where(is_text, text_id, pos_id)
    q_info = jnp.stack([pos_row * sa, pos_col * sb, q_id.astype(F32)])
    q_info = jnp.concatenate([q_info, jnp.zeros((5, patches), F32)])
    blocks = q_id.reshape(-1, QB)
    low = by_page(blocks[:, 0], starts) // BLK
    high = (by_page(blocks[:, -1], ends) + BLK - 1) // BLK
    first, kind = jnp.zeros_like(low), jnp.full_like(low, len(SIZES) - 1)
    for i in reversed(range(len(SIZES) - 1)):
        at = jnp.minimum(low, TASKS - SIZES[i])
        fits = high <= at + SIZES[i]
        first, kind = jnp.where(fits, at, first), jnp.where(fits, i, kind)
    slot = jnp.where((task >= TEXT_TASKS) & (task < TEXT_TASKS + HEADS), 2 * own, -2)
    window = jnp.stack([first, kind, jnp.full_like(first, slot)])

    def swap_heads(parts):
        own, out = parts[0], [None] * 4
        for gap in (2, 1, 3):
            swap = [(i, i ^ gap) for i in range(4)]
            out[gap] = lax.ppermute(parts[gap], "head", swap)
        return [own] + out[1:]

    hbm = pl.BlockSpec(memory_space=pltpu.HBM)
    by_head = pl.pallas_call(
        pack_self,
        out_shape=[sds((4, 32, HEADS * HS), BF)] * 4,
        in_specs=[hbm] * 4,
        out_specs=[pl.BlockSpec(memory_space=pltpu.VMEM)] * 4,
        scratch_shapes=[pltpu.SemaphoreType.DMA((4, 4))],
    )(self_queries, self_keys, self_values, self_cotangent)
    task_shape = sds((TASKS, 4, BLK, HS), BF)
    vm = pl.BlockSpec(memory_space=pltpu.VMEM)
    sent = vmem_call(pack_text, task_shape)(
        text_queries, memory_keys, memory_values, text_cotangent
    )
    by_head = swap_heads(by_head)
    sent = vmem_call(
        pack_heads,
        task_shape,
        in_specs=[vm] * 4 + [hbm],
        out_specs=hbm,
        scratch_shapes=[pltpu.VMEM((HEADS, 4, BLK, HS), BF), pltpu.SemaphoreType.DMA],
        input_output_aliases={4: 0},
    )(*by_head, sent)
    held = lax.all_to_all(sent, "seq", split_axis=0, concat_axis=0, tiled=True)
    back, slope_sum = vmem_call(
        attend,
        (sds((TASKS, 3 * BLK, HS), BF), sds((BLK, BLK), F32)),
        in_specs=[pl.BlockSpec(memory_space=pltpu.SMEM)] * 2 + [vm] * 2,
        scratch_shapes=[
            pltpu.VMEM((patches, BLK), F32),
            pltpu.VMEM((patches, BLK), F32),
            pltpu.VMEM((patches, BLK), F32),
            pltpu.VMEM((TASKS, HS, BLK), BF),
            pltpu.VMEM((patches, QB), F32),
            pltpu.VMEM((patches, QB), F32),
            pltpu.VMEM((patches, QB), BF),
            pltpu.VMEM((patches, HS), F32),
            pltpu.VMEM((patches, HS), F32),
            pltpu.VMEM((8, BLK), F32),
        ],
    )(window, pages, q_info, held)

    slope_sum = lax.psum(slope_sum, ("seq", "dp"))
    slope_sum = jnp.sum(slope_sum[: 2 * HEADS], axis=1).reshape(HEADS, 2).T
    slope_grad = slope_sum / (slopes * (LOG2E * -patches))
    back = lax.all_to_all(back, "seq", split_axis=0, concat_axis=0, tiled=True)
    text_dq, mem_dk, mem_dv, self_out = vmem_call(
        unpack_tasks,
        (
            sds(text_queries.shape, BF),
            sds(memory_keys.shape, BF),
            sds(memory_values.shape, BF),
            sds((4, 3, 32, HEADS * HS), BF),
        ),
    )(back)
    self_out = lax.all_to_all(self_out, "head", split_axis=0, concat_axis=0, tiled=True)
    shape = sds(self_queries.shape, BF)
    self_dq, self_dk, self_dv = vmem_call(unpack_self, (shape, shape, shape))(self_out)
    return self_dq, self_dk, self_dv, slope_grad, text_dq, mem_dk, mem_dv


def solution(mesh):
    rows = P("dp", ("seq", "head"), None)
    cols = P("dp", "seq", "head")
    in_specs = (rows,) * 4 + (cols,) * 4 + (P(None, "head"),) + (P("dp", None),) * 3
    out_specs = (rows,) * 3 + (P(None, "head"),) + (cols,) * 3
    return jax.shard_map(local, mesh=mesh, in_specs=in_specs, out_specs=out_specs, check_vma=False)
```

```python
import functools
import jax
import jax.numpy as jnp
from jax import lax
from jax.experimental import pallas as pl
from jax.experimental.pallas import tpu as pltpu
from jax.sharding import PartitionSpec as P

MASK_FILL = -1e30
LOG2E = 1.4426950408889634
BF = jnp.bfloat16
F32 = jnp.float32

HEADS = 5
TEXT_TASKS = 10
TASKS = 16
BLK = 128
HS = 128
QB = 256
SIZES = (5, 7, 9, 11, 13, 16)


def vmem_call(body, out_shapes, **kw):
    return pl.pallas_call(
        body,
        out_shape=out_shapes,
        compiler_params=pltpu.CompilerParams(vmem_limit_bytes=24 * 2**20),
        **kw,
    )


def pack_self(q_ref, k_ref, v_ref, g_ref, *refs):
    outs, sems = refs[:4], refs[4]
    me = lax.axis_index("head")
    width = HEADS * HS
    copies = []
    for gap in (2, 1, 3, 0):
        at = pl.ds(pl.multiple_of((me ^ gap) * width, HS), width)
        for a, ref in enumerate((q_ref, k_ref, v_ref, g_ref)):
            copies.append(
                pltpu.make_async_copy(ref.at[0, :, at], outs[gap].at[a], sems.at[gap, a])
            )
            copies[-1].start()
    for copy in copies:
        copy.wait()


def pack_text(tq_ref, mk_ref, mv_ref, tg_ref, out_ref):
    for h in range(HEADS):
        cols = slice(h * HS, (h + 1) * HS)
        for j in range(2):
            t = 2 * h + j
            rows = slice(j * BLK, (j + 1) * BLK)
            out_ref[t, 0] = tq_ref[0, rows, cols]
            out_ref[t, 1] = mk_ref[0, :, cols]
            out_ref[t, 2] = mv_ref[0, :, cols]
            out_ref[t, 3] = tg_ref[0, rows, cols]
    out_ref[TEXT_TASKS:] = jnp.zeros((TASKS - TEXT_TASKS, 4, BLK, HS), BF)


def pack_heads(s0_ref, s1_ref, s2_ref, s3_ref, text_ref, out_ref, buf, sem):
    me = lax.axis_index("head")
    for h in range(HEADS):
        cols = slice(h * HS, (h + 1) * HS)
        for gap, ref in enumerate((s0_ref, s1_ref, s2_ref, s3_ref)):
            at = pl.ds(pl.multiple_of((me ^ gap) * 32, 32), 32)
            for a in range(4):
                buf[h, a, at] = ref[a, :, cols]
    copy = pltpu.make_async_copy(buf, out_ref.at[pl.ds(TEXT_TASKS, HEADS)], sem)
    copy.start()
    copy.wait()


def unpack_tasks(in_ref, tq_ref, mk_ref, mv_ref, slope_ref, self_ref):
    k, v = (slice(i * BLK, (i + 1) * BLK) for i in (1, 2))
    slope_ref[...] = jnp.zeros_like(slope_ref)
    for h in range(HEADS):
        cols = slice(h * HS, (h + 1) * HS)
        for a in range(3):
            for x in range(4):
                at = a * BLK + x * 32
                self_ref[x, a, :, cols] = in_ref[TEXT_TASKS + h, at : at + 32]
        for j in range(2):
            tq_ref[0, j * BLK : (j + 1) * BLK, cols] = in_ref[2 * h + j, :BLK]
        mk = in_ref[2 * h, k].astype(F32) + in_ref[2 * h + 1, k].astype(F32)
        mv = in_ref[2 * h, v].astype(F32) + in_ref[2 * h + 1, v].astype(F32)
        mk_ref[0, :, cols] = mk.astype(BF)
        mv_ref[0, :, cols] = mv.astype(BF)
        pieces = in_ref[TEXT_TASKS + h, 3 * BLK :].astype(F32)
        for i in range(2):
            whole = pieces[3 * i : 3 * i + 1] + pieces[3 * i + 1 : 3 * i + 2]
            slope_ref[i, h : h + 1] = whole + pieces[3 * i + 2 : 3 * i + 3]


def unpack_self(in_ref, q_ref, k_ref, v_ref):
    width = HEADS * HS
    for x in range(4):
        for a, ref in enumerate((q_ref, k_ref, v_ref)):
            ref[0, :, x * width : (x + 1) * width] = in_ref[x, a]


def attend(
    win_ref, page_ref, qi_ref, in_ref, out_ref,
    ka_ref, kb_ref, kp_ref, kt_buf, t_buf, d_buf, ds_buf, dk_acc, dv_acc, slope_ref,
):
    inv_root = HS ** (-0.5)
    blocks = TASKS * BLK // QB
    per = QB // BLK
    for s in range(TASKS):
        here = slice(s * BLK, (s + 1) * BLK)
        kt_buf[s] = in_ref[s, 1].T
        pos = (lax.broadcasted_iota(jnp.int32, (BLK, BLK), 0) + s * BLK).astype(F32)
        begin, width, inv, page = (jnp.full((BLK, BLK), v, F32) for v in (0.0, page_ref[3, 0], page_ref[4, 0], 0.0))
        for i in range(1, 4):
            later = pos >= page_ref[2, i]
            begin = jnp.where(later, page_ref[2, i], begin)
            width = jnp.where(later, page_ref[3, i], width)
            inv = jnp.where(later, page_ref[4, i], inv)
            page = jnp.where(later, float(i), page)
        off = pos - begin
        row = jnp.floor((off + 0.5) * inv)
        ka_ref[here] = row * page_ref[0, 0]
        kb_ref[here] = (off - row * width) * page_ref[1, 0]
        kp_ref[here] = page
    dk_acc[...] = jnp.zeros_like(dk_acc)
    dv_acc[...] = jnp.zeros_like(dv_acc)
    slope_ref[...] = jnp.zeros_like(slope_ref)
    nt = (((1,), (1,)), ((), ()))
    tn = (((0,), (0,)), ((), ()))

    def wide_lanes(tile):
        return jnp.concatenate([tile] * per, axis=1)

    def fold(x, op):
        return op(x.reshape(BLK // 8, 8, QB), axis=0)

    def work(b, first, tiles):
        start = first * BLK
        q = jnp.concatenate([in_ref[per * b + i, 0] for i in range(per)], axis=0)
        g = jnp.concatenate([in_ref[per * b + i, 3] for i in range(per)], axis=0)
        at = pl.ds(pl.multiple_of(b * QB, QB), QB)
        qa, qb, qp = (qi_ref[i : i + 1, at] for i in range(3))

        def rows(t):
            return pl.ds(pl.multiple_of(start + t * BLK, BLK), BLK)

        top = jnp.full((8, QB), -jnp.inf, F32)
        for t in range(tiles):
            r = rows(t)
            s = lax.dot_general(in_ref[first + t, 1], q, nt, preferred_element_type=F32)
            d_buf[t * BLK : (t + 1) * BLK] = lax.dot_general(
                in_ref[first + t, 2], g, nt, preferred_element_type=F32
            )
            gap = jnp.abs(wide_lanes(ka_ref[r]) - qa) + jnp.abs(wide_lanes(kb_ref[r]) - qb)
            logit = jnp.where(
                wide_lanes(kp_ref[r]) == qp, s * (inv_root * LOG2E) - gap, MASK_FILL
            )
            t_buf[t * BLK : (t + 1) * BLK] = logit
            top = jnp.maximum(top, fold(logit, jnp.max))
        top = jnp.max(top, axis=0, keepdims=True)
        total = jnp.zeros((8, QB), F32)
        dot = jnp.zeros((8, QB), F32)
        for t in range(tiles):
            here = slice(t * BLK, (t + 1) * BLK)
            e = jnp.exp2(t_buf[here] - top)
            total += fold(e, jnp.sum)
            dot += fold(e * d_buf[here], jnp.sum)
        total = jnp.sum(total, axis=0, keepdims=True)
        inv = 1.0 / total
        norm = top + jnp.log2(total)
        delta = jnp.sum(dot, axis=0, keepdims=True) * inv
        sa = jnp.zeros((8, QB), F32)
        sb = jnp.zeros((8, QB), F32)
        for t in range(tiles):
            here = slice(t * BLK, (t + 1) * BLK)
            r = rows(t)
            p = jnp.exp2(t_buf[here] - norm)
            ds = p * (d_buf[here] - delta)
            p_b = p.astype(BF)
            ds_b = ds.astype(BF)
            ds_buf[here] = ds_b
            sa += fold(ds * jnp.abs(wide_lanes(ka_ref[r]) - qa), jnp.sum)
            sb += fold(ds * jnp.abs(wide_lanes(kb_ref[r]) - qb), jnp.sum)
            dv_acc[r] += jnp.dot(p_b, g, preferred_element_type=F32)
            dk_acc[r] += jnp.dot(ds_b, q, preferred_element_type=F32)
        kt = jnp.concatenate([kt_buf[first + t] for t in range(tiles)], axis=1)
        dq = jnp.dot(kt, ds_buf[: tiles * BLK], preferred_element_type=F32).T
        dq = (dq * inv_root).astype(BF)
        for i in range(per):
            out_ref[per * b + i, :BLK] = dq[i * BLK : (i + 1) * BLK]
        for row, v in ((0, sa), (1, sb)):
            v = jnp.sum(v, axis=0, keepdims=True)
            slope_ref[row : row + 1] += sum(v[:, i * BLK : (i + 1) * BLK] for i in range(per))

    def step(b, _):
        for kind, tiles in enumerate(SIZES):

            @pl.when(win_ref[1, b] == kind)
            def _(tiles=tiles):
                work(b, win_ref[0, b], tiles)

        return 0

    lax.fori_loop(0, blocks, step, 0)
    line = lax.broadcasted_iota(jnp.int32, (16, BLK), 0)
    pieces = jnp.zeros((16, BLK), F32)
    for row in range(2):
        rest = jnp.broadcast_to(slope_ref[row : row + 1], (16, BLK))
        for i in range(3):
            piece = rest.astype(BF).astype(F32)
            rest = rest - piece
            pieces = jnp.where(line == 3 * row + i, piece, pieces)
    pieces = pieces.astype(BF)
    for s in range(TASKS):
        here = slice(s * BLK, (s + 1) * BLK)
        out_ref[s, BLK : 2 * BLK] = (dk_acc[here] * inv_root).astype(BF)
        out_ref[s, 2 * BLK : 3 * BLK] = dv_acc[here].astype(BF)
        out_ref[s, 3 * BLK :] = pieces


def local(
    self_queries, self_keys, self_values, self_cotangent,
    text_queries, memory_keys, memory_values, text_cotangent,
    slopes, page_counts, page_cols, text_page,
):
    patches = TASKS * BLK
    sds = jax.ShapeDtypeStruct
    task = lax.axis_index("seq")
    is_text = task < TEXT_TASKS

    counts, widths = page_counts[0], page_cols[0]
    ends = [counts[0]]
    for i in range(1, 4):
        ends.append(ends[-1] + counts[i])
    starts = [jnp.int32(0)] + ends[:-1]

    def by_page(ids, per_page):
        out = jnp.broadcast_to(per_page[3], ids.shape)
        for i in (2, 1, 0):
            out = jnp.where(ids == i, per_page[i], out)
        return out

    def layout(pos):
        ids = sum((pos >= e).astype(jnp.int32) for e in ends[:3])
        width = by_page(ids, [widths[i] for i in range(4)])
        off = (pos - by_page(ids, starts)).astype(F32)
        row = jnp.floor((off + 0.5) / width.astype(F32))
        return ids, row, off - row * width.astype(F32)

    own = jnp.clip(task - TEXT_TASKS, 0, HEADS - 1)
    slope = jnp.where(is_text, 0.0, lax.dynamic_slice_in_dim(slopes, own, 1, 1)[:, 0])
    sa, sb = slope[0] * LOG2E, slope[1] * LOG2E
    as_row = lambda values: jnp.stack([jnp.asarray(v, F32) for v in values])
    pages = jnp.stack(
        [
            as_row([sa] * 4),
            as_row([sb] * 4),
            as_row(starts),
            widths.astype(F32),
            1.0 / widths.astype(F32),
        ]
    )
    pos_id, pos_row, pos_col = layout(jnp.arange(patches, dtype=jnp.int32))
    halves = text_page[0].reshape(TASKS, 2, BLK)
    text_id = lax.dynamic_index_in_dim(halves, task % 2, 1, keepdims=False).reshape(-1)
    q_id = jnp.where(is_text, text_id, pos_id)
    q_info = jnp.stack([pos_row * sa, pos_col * sb, q_id.astype(F32)])
    q_info = jnp.concatenate([q_info, jnp.zeros((5, patches), F32)])
    blocks = q_id.reshape(-1, QB)
    low = by_page(blocks[:, 0], starts) // BLK
    high = (by_page(blocks[:, -1], ends) + BLK - 1) // BLK
    first, kind = jnp.zeros_like(low), jnp.full_like(low, len(SIZES) - 1)
    for i in reversed(range(len(SIZES) - 1)):
        at = jnp.minimum(low, TASKS - SIZES[i])
        fits = high <= at + SIZES[i]
        first, kind = jnp.where(fits, at, first), jnp.where(fits, i, kind)
    window = jnp.stack([first, kind])

    def swap_heads(parts):
        own, out = parts[0], [None] * 4
        for gap in (2, 1, 3):
            swap = [(i, i ^ gap) for i in range(4)]
            out[gap] = lax.ppermute(parts[gap], "head", swap)
        return [own] + out[1:]

    hbm = pl.BlockSpec(memory_space=pltpu.HBM)
    by_head = pl.pallas_call(
        pack_self,
        out_shape=[sds((4, 32, HEADS * HS), BF)] * 4,
        in_specs=[hbm] * 4,
        out_specs=[pl.BlockSpec(memory_space=pltpu.VMEM)] * 4,
        scratch_shapes=[pltpu.SemaphoreType.DMA((4, 4))],
    )(self_queries, self_keys, self_values, self_cotangent)
    task_shape = sds((TASKS, 4, BLK, HS), BF)
    vm = pl.BlockSpec(memory_space=pltpu.VMEM)
    sent = vmem_call(pack_text, task_shape)(
        text_queries, memory_keys, memory_values, text_cotangent
    )
    by_head = swap_heads(by_head)
    sent = vmem_call(
        pack_heads,
        task_shape,
        in_specs=[vm] * 4 + [hbm],
        out_specs=hbm,
        scratch_shapes=[pltpu.VMEM((HEADS, 4, BLK, HS), BF), pltpu.SemaphoreType.DMA],
        input_output_aliases={4: 0},
    )(*by_head, sent)
    held = lax.all_to_all(sent, "seq", split_axis=0, concat_axis=0, tiled=True)
    back = vmem_call(
        attend,
        sds((TASKS, 3 * BLK + 16, HS), BF),
        in_specs=[pl.BlockSpec(memory_space=pltpu.SMEM)] * 2 + [vm] * 2,
        scratch_shapes=[
            pltpu.VMEM((patches, BLK), F32),
            pltpu.VMEM((patches, BLK), F32),
            pltpu.VMEM((patches, BLK), F32),
            pltpu.VMEM((TASKS, HS, BLK), BF),
            pltpu.VMEM((patches, QB), F32),
            pltpu.VMEM((patches, QB), F32),
            pltpu.VMEM((patches, QB), BF),
            pltpu.VMEM((patches, HS), F32),
            pltpu.VMEM((patches, HS), F32),
            pltpu.VMEM((8, BLK), F32),
        ],
    )(window, pages, q_info, held)

    back = lax.all_to_all(back, "seq", split_axis=0, concat_axis=0, tiled=True)
    text_dq, mem_dk, mem_dv, slope_sum, self_out = vmem_call(
        unpack_tasks,
        (
            sds(text_queries.shape, BF),
            sds(memory_keys.shape, BF),
            sds(memory_values.shape, BF),
            sds((2, 8, BLK), F32),
            sds((4, 3, 32, HEADS * HS), BF),
        ),
    )(back)
    self_out = lax.all_to_all(self_out, "head", split_axis=0, concat_axis=0, tiled=True)
    near, far, last = (
        lax.ppermute(slope_sum, "dp", [(i, i ^ gap) for i in range(4)])
        for gap in (1, 2, 3)
    )
    slope_sum = (slope_sum + near) + (far + last)
    slope_sum = jnp.sum(slope_sum[:, :HEADS], axis=2)
    slope_grad = slope_sum / (slopes * (LOG2E * -patches))
    shape = sds(self_queries.shape, BF)
    self_dq, self_dk, self_dv = vmem_call(unpack_self, (shape, shape, shape))(self_out)
    return self_dq, self_dk, self_dv, slope_grad, text_dq, mem_dk, mem_dv


def solution(mesh):
    rows = P("dp", ("seq", "head"), None)
    cols = P("dp", "seq", "head")
    in_specs = (rows,) * 4 + (cols,) * 4 + (P(None, "head"),) + (P("dp", None),) * 3
    out_specs = (rows,) * 3 + (P(None, "head"),) + (cols,) * 3
    return jax.shard_map(local, mesh=mesh, in_specs=in_specs, out_specs=out_specs, check_vma=False)
```

```python
import functools
import jax
import jax.numpy as jnp
from jax import lax
from jax.experimental import pallas as pl
from jax.experimental.pallas import tpu as pltpu
from jax.sharding import PartitionSpec as P

MASK_FILL = -1e30
LOG2E = 1.4426950408889634
BF = jnp.bfloat16
F32 = jnp.float32

HEADS = 5
TEXT_TASKS = 10
TASKS = 16
BLK = 128
HS = 128
QB = 256
SIZES = (4, 6, 8, 9, 10, 12, 14, 16)


def vmem_call(body, out_shapes, **kw):
    return pl.pallas_call(
        body,
        out_shape=out_shapes,
        compiler_params=pltpu.CompilerParams(vmem_limit_bytes=24 * 2**20),
        **kw,
    )


def pack_self(q_ref, k_ref, v_ref, g_ref, *refs):
    outs, sems = refs[:4], refs[4]
    me = lax.axis_index("head")
    width = HEADS * HS
    copies = []
    for gap in (2, 1, 3, 0):
        at = pl.ds(pl.multiple_of((me ^ gap) * width, HS), width)
        for a, ref in enumerate((q_ref, k_ref, v_ref, g_ref)):
            copies.append(
                pltpu.make_async_copy(ref.at[0, :, at], outs[gap].at[a], sems.at[gap, a])
            )
            copies[-1].start()
    for copy in copies:
        copy.wait()


def pack_text(tq_ref, mk_ref, mv_ref, tg_ref, out_ref):
    for h in range(HEADS):
        cols = slice(h * HS, (h + 1) * HS)
        for j in range(2):
            t = 2 * h + j
            rows = slice(j * BLK, (j + 1) * BLK)
            out_ref[t, 0] = tq_ref[0, rows, cols]
            out_ref[t, 1] = mk_ref[0, :, cols]
            out_ref[t, 2] = mv_ref[0, :, cols]
            out_ref[t, 3] = tg_ref[0, rows, cols]
    out_ref[TEXT_TASKS:] = jnp.zeros((TASKS - TEXT_TASKS, 4, BLK, HS), BF)


def pack_heads(s0_ref, s1_ref, s2_ref, s3_ref, text_ref, out_ref, buf, sem):
    me = lax.axis_index("head")
    for h in range(HEADS):
        cols = slice(h * HS, (h + 1) * HS)
        for gap, ref in enumerate((s0_ref, s1_ref, s2_ref, s3_ref)):
            at = pl.ds(pl.multiple_of((me ^ gap) * 32, 32), 32)
            for a in range(4):
                buf[h, a, at] = ref[a, :, cols]
    copy = pltpu.make_async_copy(buf, out_ref.at[pl.ds(TEXT_TASKS, HEADS)], sem)
    copy.start()
    copy.wait()


def unpack_tasks(in_ref, tq_ref, mk_ref, mv_ref, slope_ref, self_ref):
    k, v = (slice(i * BLK, (i + 1) * BLK) for i in (1, 2))
    slope_ref[...] = jnp.zeros_like(slope_ref)
    for h in range(HEADS):
        cols = slice(h * HS, (h + 1) * HS)
        for a in range(3):
            for x in range(4):
                at = a * BLK + x * 32
                self_ref[x, a, :, cols] = in_ref[TEXT_TASKS + h, at : at + 32]
        for j in range(2):
            tq_ref[0, j * BLK : (j + 1) * BLK, cols] = in_ref[2 * h + j, :BLK]
        mk = in_ref[2 * h, k].astype(F32) + in_ref[2 * h + 1, k].astype(F32)
        mv = in_ref[2 * h, v].astype(F32) + in_ref[2 * h + 1, v].astype(F32)
        mk_ref[0, :, cols] = mk.astype(BF)
        mv_ref[0, :, cols] = mv.astype(BF)
        pieces = in_ref[TEXT_TASKS + h, 3 * BLK :].astype(F32)
        for i in range(2):
            whole = pieces[3 * i : 3 * i + 1] + pieces[3 * i + 1 : 3 * i + 2]
            slope_ref[i, h : h + 1] = whole + pieces[3 * i + 2 : 3 * i + 3]


def unpack_self(in_ref, q_ref, k_ref, v_ref):
    width = HEADS * HS
    for x in range(4):
        for a, ref in enumerate((q_ref, k_ref, v_ref)):
            ref[0, :, x * width : (x + 1) * width] = in_ref[x, a]


def attend(
    win_ref, page_ref, qi_ref, in_ref, out_ref,
    ka_ref, kb_ref, kp_ref, kt_buf, t_buf, d_buf, ds_buf, dk_acc, dv_acc, slope_ref,
):
    inv_root = HS ** (-0.5)
    blocks = TASKS * BLK // QB
    per = QB // BLK
    for s in range(TASKS):
        here = slice(s * BLK, (s + 1) * BLK)
        kt_buf[s] = in_ref[s, 1].T
        pos = (lax.broadcasted_iota(jnp.int32, (BLK, BLK), 0) + s * BLK).astype(F32)
        begin, width, inv, page = (jnp.full((BLK, BLK), v, F32) for v in (0.0, page_ref[3, 0], page_ref[4, 0], 0.0))
        for i in range(1, 4):
            later = pos >= page_ref[2, i]
            begin = jnp.where(later, page_ref[2, i], begin)
            width = jnp.where(later, page_ref[3, i], width)
            inv = jnp.where(later, page_ref[4, i], inv)
            page = jnp.where(later, float(i), page)
        off = pos - begin
        row = jnp.floor((off + 0.5) * inv)
        ka_ref[here] = row * page_ref[0, 0]
        kb_ref[here] = (off - row * width) * page_ref[1, 0]
        kp_ref[here] = page
    dk_acc[...] = jnp.zeros_like(dk_acc)
    dv_acc[...] = jnp.zeros_like(dv_acc)
    slope_ref[...] = jnp.zeros_like(slope_ref)
    nt = (((1,), (1,)), ((), ()))
    tn = (((0,), (0,)), ((), ()))

    def wide_lanes(tile):
        return jnp.concatenate([tile] * per, axis=1)

    def fold(x, op):
        return op(x.reshape(BLK // 8, 8, QB), axis=0)

    def work(b, first, tiles):
        start = first * BLK
        q = jnp.concatenate([in_ref[per * b + i, 0] for i in range(per)], axis=0)
        g = jnp.concatenate([in_ref[per * b + i, 3] for i in range(per)], axis=0)
        at = pl.ds(pl.multiple_of(b * QB, QB), QB)
        qa, qb, qp = (qi_ref[i : i + 1, at] for i in range(3))

        def rows(t):
            return pl.ds(pl.multiple_of(start + t * BLK, BLK), BLK)

        top = jnp.full((8, QB), -jnp.inf, F32)
        for t in range(tiles):
            r = rows(t)
            s = lax.dot_general(in_ref[first + t, 1], q, nt, preferred_element_type=F32)
            d_buf[t * BLK : (t + 1) * BLK] = lax.dot_general(
                in_ref[first + t, 2], g, nt, preferred_element_type=F32
            )
            gap = jnp.abs(wide_lanes(ka_ref[r]) - qa) + jnp.abs(wide_lanes(kb_ref[r]) - qb)
            logit = jnp.where(
                wide_lanes(kp_ref[r]) == qp, s * (inv_root * LOG2E) - gap, MASK_FILL
            )
            t_buf[t * BLK : (t + 1) * BLK] = logit
            top = jnp.maximum(top, fold(logit, jnp.max))
        top = jnp.max(top, axis=0, keepdims=True)
        total = jnp.zeros((8, QB), F32)
        dot = jnp.zeros((8, QB), F32)
        for t in range(tiles):
            here = slice(t * BLK, (t + 1) * BLK)
            e = jnp.exp2(t_buf[here] - top)
            total += fold(e, jnp.sum)
            dot += fold(e * d_buf[here], jnp.sum)
        total = jnp.sum(total, axis=0, keepdims=True)
        inv = 1.0 / total
        norm = top + jnp.log2(total)
        delta = jnp.sum(dot, axis=0, keepdims=True) * inv
        sa = jnp.zeros((8, QB), F32)
        sb = jnp.zeros((8, QB), F32)
        for t in range(tiles):
            here = slice(t * BLK, (t + 1) * BLK)
            r = rows(t)
            p = jnp.exp2(t_buf[here] - norm)
            ds = p * (d_buf[here] - delta)
            p_b = p.astype(BF)
            ds_b = ds.astype(BF)
            ds_buf[here] = ds_b
            sa += fold(ds * jnp.abs(wide_lanes(ka_ref[r]) - qa), jnp.sum)
            sb += fold(ds * jnp.abs(wide_lanes(kb_ref[r]) - qb), jnp.sum)
            dv_acc[r] += jnp.dot(p_b, g, preferred_element_type=F32)
            dk_acc[r] += jnp.dot(ds_b, q, preferred_element_type=F32)
        kt = jnp.concatenate([kt_buf[first + t] for t in range(tiles)], axis=1)
        dq = jnp.dot(kt, ds_buf[: tiles * BLK], preferred_element_type=F32).T
        dq = (dq * inv_root).astype(BF)
        for i in range(per):
            out_ref[per * b + i, :BLK] = dq[i * BLK : (i + 1) * BLK]
        for row, v in ((0, sa), (1, sb)):
            v = jnp.sum(v, axis=0, keepdims=True)
            slope_ref[row : row + 1] += sum(v[:, i * BLK : (i + 1) * BLK] for i in range(per))

    def step(b, _):
        for kind, tiles in enumerate(SIZES):

            @pl.when(win_ref[1, b] == kind)
            def _(tiles=tiles):
                work(b, win_ref[0, b], tiles)

        return 0

    lax.fori_loop(0, blocks, step, 0)
    line = lax.broadcasted_iota(jnp.int32, (16, BLK), 0)
    pieces = jnp.zeros((16, BLK), F32)
    for row in range(2):
        rest = jnp.broadcast_to(slope_ref[row : row + 1], (16, BLK))
        for i in range(3):
            piece = rest.astype(BF).astype(F32)
            rest = rest - piece
            pieces = jnp.where(line == 3 * row + i, piece, pieces)
    pieces = pieces.astype(BF)
    for s in range(TASKS):
        here = slice(s * BLK, (s + 1) * BLK)
        out_ref[s, BLK : 2 * BLK] = (dk_acc[here] * inv_root).astype(BF)
        out_ref[s, 2 * BLK : 3 * BLK] = dv_acc[here].astype(BF)
        out_ref[s, 3 * BLK :] = pieces


def local(
    self_queries, self_keys, self_values, self_cotangent,
    text_queries, memory_keys, memory_values, text_cotangent,
    slopes, page_counts, page_cols, text_page,
):
    patches = TASKS * BLK
    sds = jax.ShapeDtypeStruct
    task = lax.axis_index("seq")
    is_text = task < TEXT_TASKS

    counts, widths = page_counts[0], page_cols[0]
    ends = [counts[0]]
    for i in range(1, 4):
        ends.append(ends[-1] + counts[i])
    starts = [jnp.int32(0)] + ends[:-1]

    def by_page(ids, per_page):
        out = jnp.broadcast_to(per_page[3], ids.shape)
        for i in (2, 1, 0):
            out = jnp.where(ids == i, per_page[i], out)
        return out

    def layout(pos):
        ids = sum((pos >= e).astype(jnp.int32) for e in ends[:3])
        width = by_page(ids, [widths[i] for i in range(4)])
        off = (pos - by_page(ids, starts)).astype(F32)
        row = jnp.floor((off + 0.5) / width.astype(F32))
        return ids, row, off - row * width.astype(F32)

    own = jnp.clip(task - TEXT_TASKS, 0, HEADS - 1)
    slope = jnp.where(is_text, 0.0, lax.dynamic_slice_in_dim(slopes, own, 1, 1)[:, 0])
    sa, sb = slope[0] * LOG2E, slope[1] * LOG2E
    as_row = lambda values: jnp.stack([jnp.asarray(v, F32) for v in values])
    pages = jnp.stack(
        [
            as_row([sa] * 4),
            as_row([sb] * 4),
            as_row(starts),
            widths.astype(F32),
            1.0 / widths.astype(F32),
        ]
    )
    pos_id, pos_row, pos_col = layout(jnp.arange(patches, dtype=jnp.int32))
    halves = text_page[0].reshape(TASKS, 2, BLK)
    text_id = lax.dynamic_index_in_dim(halves, task % 2, 1, keepdims=False).reshape(-1)
    q_id = jnp.where(is_text, text_id, pos_id)
    q_info = jnp.stack([pos_row * sa, pos_col * sb, q_id.astype(F32)])
    q_info = jnp.concatenate([q_info, jnp.zeros((5, patches), F32)])
    blocks = q_id.reshape(-1, QB)
    low = by_page(blocks[:, 0], starts) // BLK
    high = (by_page(blocks[:, -1], ends) + BLK - 1) // BLK
    first, kind = jnp.zeros_like(low), jnp.full_like(low, len(SIZES) - 1)
    for i in reversed(range(len(SIZES) - 1)):
        at = jnp.minimum(low, TASKS - SIZES[i])
        fits = high <= at + SIZES[i]
        first, kind = jnp.where(fits, at, first), jnp.where(fits, i, kind)
    window = jnp.stack([first, kind])

    def swap_heads(parts):
        own, out = parts[0], [None] * 4
        for gap in (2, 1, 3):
            swap = [(i, i ^ gap) for i in range(4)]
            out[gap] = lax.ppermute(parts[gap], "head", swap)
        return [own] + out[1:]

    hbm = pl.BlockSpec(memory_space=pltpu.HBM)
    by_head = pl.pallas_call(
        pack_self,
        out_shape=[sds((4, 32, HEADS * HS), BF)] * 4,
        in_specs=[hbm] * 4,
        out_specs=[pl.BlockSpec(memory_space=pltpu.VMEM)] * 4,
        scratch_shapes=[pltpu.SemaphoreType.DMA((4, 4))],
    )(self_queries, self_keys, self_values, self_cotangent)
    task_shape = sds((TASKS, 4, BLK, HS), BF)
    vm = pl.BlockSpec(memory_space=pltpu.VMEM)
    sent = vmem_call(pack_text, task_shape)(
        text_queries, memory_keys, memory_values, text_cotangent
    )
    by_head = swap_heads(by_head)
    sent = vmem_call(
        pack_heads,
        task_shape,
        in_specs=[vm] * 4 + [hbm],
        out_specs=hbm,
        scratch_shapes=[pltpu.VMEM((HEADS, 4, BLK, HS), BF), pltpu.SemaphoreType.DMA],
        input_output_aliases={4: 0},
    )(*by_head, sent)
    held = lax.all_to_all(sent, "seq", split_axis=0, concat_axis=0, tiled=True)
    back = vmem_call(
        attend,
        sds((TASKS, 3 * BLK + 16, HS), BF),
        in_specs=[pl.BlockSpec(memory_space=pltpu.SMEM)] * 2 + [vm] * 2,
        scratch_shapes=[
            pltpu.VMEM((patches, BLK), F32),
            pltpu.VMEM((patches, BLK), F32),
            pltpu.VMEM((patches, BLK), F32),
            pltpu.VMEM((TASKS, HS, BLK), BF),
            pltpu.VMEM((patches, QB), F32),
            pltpu.VMEM((patches, QB), F32),
            pltpu.VMEM((patches, QB), BF),
            pltpu.VMEM((patches, HS), F32),
            pltpu.VMEM((patches, HS), F32),
            pltpu.VMEM((8, BLK), F32),
        ],
    )(window, pages, q_info, held)

    back = lax.all_to_all(back, "seq", split_axis=0, concat_axis=0, tiled=True)
    text_dq, mem_dk, mem_dv, slope_sum, self_out = vmem_call(
        unpack_tasks,
        (
            sds(text_queries.shape, BF),
            sds(memory_keys.shape, BF),
            sds(memory_values.shape, BF),
            sds((2, 8, BLK), F32),
            sds((4, 3, 32, HEADS * HS), BF),
        ),
    )(back)
    self_out = lax.all_to_all(self_out, "head", split_axis=0, concat_axis=0, tiled=True)
    near, far, last = (
        lax.ppermute(slope_sum, "dp", [(i, i ^ gap) for i in range(4)])
        for gap in (1, 2, 3)
    )
    slope_sum = (slope_sum + near) + (far + last)
    slope_sum = jnp.sum(slope_sum[:, :HEADS], axis=2)
    slope_grad = slope_sum / (slopes * (LOG2E * -patches))
    shape = sds(self_queries.shape, BF)
    self_dq, self_dk, self_dv = vmem_call(unpack_self, (shape, shape, shape))(self_out)
    return self_dq, self_dk, self_dv, slope_grad, text_dq, mem_dk, mem_dv


def solution(mesh):
    rows = P("dp", ("seq", "head"), None)
    cols = P("dp", "seq", "head")
    in_specs = (rows,) * 4 + (cols,) * 4 + (P(None, "head"),) + (P("dp", None),) * 3
    out_specs = (rows,) * 3 + (P(None, "head"),) + (cols,) * 3
    return jax.shard_map(local, mesh=mesh, in_specs=in_specs, out_specs=out_specs, check_vma=False)
```
